512 devices in a mesh: gx: 32 (over y, x, core), gy: 16 (over z).
Axes of the slice: x: 4, y: 4, z: 16, core: 2. Of those that a mesh axis runs over, the one named last changes fastest.
Arguments:
- basis: float32 [32, 256, 128, 256], P(None, 'gx', 'gy'), may hold values from -6 to 6
- rhs: float32 [256, 128, 256], P('gx', 'gy'), may hold values from -12 to 12
- extra_diag: float32 [256, 128, 256], P('gx', 'gy'), may hold values from 0.02 to 0.5
- coeff: float32 [3, 256, 128, 256], P(None, 'gx', 'gy'), may hold values from 0.3 to 3
Outputs:
- guess: float32 [256, 128, 256], P('gx', 'gy')
- stepped: float32 [256, 128, 256], P('gx', 'gy')
The draws below stay inside these ranges and needn't reach their ends.
All inputs are finite; a program needn't handle non-finite values.
Results may differ from the reference program's by a relative error of at most 0.0003.
Values sent between devices are 32-bit elements; how exact they have to be, the bound alone decides.
A program may use at most 64 MiB of HBM per device.

```python
import math
import jax
import jax.numpy as jnp
from jax import lax

NZ = 256
NV = 32
NX = 256
NY = 128


def shared_fields(key):
    common_key = jax.random.fold_in(key, 101)
    latent_key = jax.random.fold_in(key, 102)
    own_key = jax.random.fold_in(key, 103)
    mixing_key = jax.random.fold_in(key, 104)
    factor_key = jax.random.fold_in(key, 105)
    noise_key = jax.random.fold_in(key, 106)
    latent_count = 8
    common = jnp.clip(jax.random.normal(common_key, (NX, NY, NZ), jnp.float32), -4.0, 4.0)
    latent = jnp.clip(jax.random.normal(latent_key, (latent_count, NX, NY, NZ), jnp.float32), -4.0, 4.0)
    own = jnp.clip(jax.random.normal(own_key, (NV, NX, NY, NZ), jnp.float32), -4.0, 4.0)
    noise_scale = 0.6
    mixing = jnp.clip(jax.random.normal(mixing_key, (NV, latent_count), jnp.float32), -3.0, 3.0) / math.sqrt(latent_count)
    vectors = common[None] + jnp.tensordot(mixing, latent, axes=1) + own
    vectors = jnp.clip(vectors, -6.0, 6.0)
    factors = jnp.clip(jax.random.normal(factor_key, (NV,), jnp.float32), -3.0, 3.0)
    noise = jnp.clip(jax.random.normal(noise_key, (NX, NY, NZ), jnp.float32), -6.0, 6.0)
    right = jnp.tensordot(factors, vectors, axes=1) / math.sqrt(NV) + noise_scale * noise
    return (vectors, jnp.clip(right, -12.0, 12.0))


def draw_basis(key, part):
    return shared_fields(key)[0]


def draw_rhs(key, part):
    return shared_fields(key)[1]


def block_levels(rng, extent, shards, smallest, high):
    factor_of = 1.0
    for axis_at, blocks in shards:
        steps = jax.random.uniform(jax.random.fold_in(jax.random.fold_in(rng, 6), axis_at), (blocks,), jnp.float32, smallest / len(shards), high / len(shards))
        factor_of = factor_of * jnp.repeat(jnp.exp(steps), extent[axis_at] // blocks).reshape((-1,) + (1,) * (len(extent) - 1 - axis_at))
    return factor_of


def setup_inputs(seed: int = 0) -> dict:
    arg_keys = jax.random.split(jax.random.key(seed), 5)
    basis = draw_basis(jax.random.fold_in(arg_keys[4], 71), 0)
    rhs = draw_rhs(jax.random.fold_in(arg_keys[4], 71), 0)
    extra_diag = jnp.clip(jnp.exp(math.log(0.5) - 3.218876 * jax.random.uniform(arg_keys[2], (NX, NY, NZ), jnp.float32) ** block_levels(arg_keys[2], (NX, NY, NZ), ((0, 32), (1, 16)), -0.2, 0.2)), 0.02, 0.5)
    coeff = jnp.clip(jnp.exp(math.log(3.0) - 2.3025851 * jax.random.uniform(arg_keys[3], (3, NX, NY, NZ), jnp.float32) ** block_levels(arg_keys[3], (3, NX, NY, NZ), ((1, 32), (2, 16)), -0.2, 0.2)), 0.3, 3.0)
    return {"basis": basis, "rhs": rhs, "extra_diag": extra_diag, "coeff": coeff}


precise = lax.Precision.HIGHEST

def flux_apply(padded, coeff_pad, extra):
    center = padded[:, 1:-1, 1:-1]
    coeff_mid = coeff_pad[:, 1:-1, 1:-1]
    flux_x = coeff_mid[0] * (center - padded[:, 2:, 1:-1])
    flux_y = coeff_mid[1] * (center - padded[:, 1:-1, 2:])
    below_x = coeff_pad[0, :-2, 1:-1] * (padded[:, :-2, 1:-1] - center)
    below_y = coeff_pad[1, 1:-1, :-2] * (padded[:, 1:-1, :-2] - center)
    next_z = jnp.concatenate([center[..., 1:], jnp.zeros_like(center[..., :1])], axis=-1)
    flux_z = coeff_mid[2] * (center - next_z)
    below_z = jnp.concatenate([jnp.zeros_like(flux_z[..., :1]), flux_z[..., :-1]], axis=-1)
    return extra * center + flux_x + flux_y + flux_z - below_x - below_y - below_z

def small_solve(matrix, vector):
    lower = jnp.linalg.cholesky(matrix)
    middle = lax.linalg.triangular_solve(lower, vector[:, None], left_side=True, lower=True)
    result = lax.linalg.triangular_solve(lower, middle, left_side=True, lower=True, transpose_a=True)
    return result[:, 0]

def reference(basis, rhs, extra_diag, coeff):
    coeff_pad = jnp.pad(coeff, ((0, 0), (1, 1), (1, 1), (0, 0)))

    def apply_one(field):
        padded = jnp.pad(field, ((1, 1), (1, 1), (0, 0)))
        return flux_apply(padded[None], coeff_pad, extra_diag)[0]
    applied = lax.map(apply_one, basis)
    flat_basis = basis.reshape(NV, -1)
    gram = jnp.dot(flat_basis, applied.reshape(NV, -1).T, precision=precise)
    gram = 0.5 * (gram + gram.T)
    projected = jnp.dot(flat_basis, rhs.reshape(-1), precision=precise)
    weights = small_solve(gram, projected)
    guess = jnp.tensordot(weights, basis, axes=1, precision=precise)
    residual = rhs - apply_one(guess)
    coeff_mid = coeff_pad[:, 1:-1, 1:-1]
    below_kz = jnp.concatenate([jnp.zeros_like(coeff[2][..., :1]), coeff[2][..., :-1]], axis=-1)
    diagonal = extra_diag + coeff_mid[0] + coeff_mid[1] + coeff_mid[2] + coeff_pad[0, :-2, 1:-1] + coeff_pad[1, 1:-1, :-2] + below_kz
    direction = residual / diagonal
    applied_dir = apply_one(direction)
    correction = jnp.dot(flat_basis, applied_dir.reshape(-1), precision=precise)
    shift_coef = small_solve(gram, correction)
    update = direction - jnp.tensordot(shift_coef, basis, axes=1, precision=precise)
    applied_upd = apply_one(update)
    step_size = jnp.sum(residual * update) / jnp.sum(update * applied_upd)
    return (guess, guess + step_size * update)
```

```python
import functools

import jax
import jax.numpy as jnp
from jax import lax
from jax.experimental import pallas as pl
from jax.experimental.pallas import tpu as pltpu
from jax.sharding import PartitionSpec as P

MESH = pl.DeviceIdType.MESH
F32 = jnp.float32
BF16 = jnp.bfloat16
NV = 32
BX = 8
BY = 8
BZ = 256
HZ = 128
CHUNKS = 4
ROWS = 9


def split(value):
    high = value.astype(BF16)
    low = (value - high.astype(F32)).astype(BF16)
    return high, low


def dot_t(a, b):
    return lax.dot_general(a, b, (((1,), (1,)), ((), ())), preferred_element_type=F32)


def kernel(
    n_gx,
    n_gy,
    basis_hbm,
    rhs_hbm,
    extra_hbm,
    coeff_hbm,
    guess_hbm,
    stepped_hbm,
    v_ref,
    rhs_ref,
    ext_ref,
    cf_ref,
    vh,
    vl,
    ah,
    al,
    fh,
    fl,
    gh,
    gl,
    pylo,
    pyhi,
    hxlo,
    hxup,
    hylo,
    hyup,
    cxm,
    cym,
    cpack,
    cxlo,
    cylo,
    proj_acc,
    prod,
    wb,
    g_ref,
    d_ref,
    o_ref,
    dplo,
    dphi,
    dxlo,
    dxup,
    dylo,
    dyup,
    src1,
    src2,
    a1c,
    a1x,
    a1z,
    a2c,
    a2x,
    a2z,
    load_sem,
    out_sem,
    hs_send,
    hs_recv,
    ar_send,
    ar_recv,
):
    ix = lax.axis_index("gx")
    iy = lax.axis_index("gy")
    core = ix % 2
    xy = ix // 2
    n_xy = n_gx // 2
    up_x = ((ix + 1) % n_gx, iy)
    lo_x = ((ix + n_gx - 1) % n_gx, iy)
    up_y = (ix, (iy + 1) % n_gy)
    lo_y = (ix, (iy + n_gy - 1) % n_gy)
    core_peers = [(xy * 2 + (core + 1) % 2, iy)]
    xy_peers = [(((xy + t) % n_xy) * 2 + core, iy) for t in range(1, n_xy)]
    z_peers = [(ix, (iy + t) % n_gy) for t in range(1, n_gy)]
    first_x, last_x = ix == 0, ix == n_gx - 1
    first_y, last_y = iy == 0, iy == n_gy - 1

    per = NV // CHUNKS
    loads = [
        pltpu.make_async_copy(coeff_hbm, cf_ref, load_sem.at[CHUNKS]),
        pltpu.make_async_copy(rhs_hbm, rhs_ref, load_sem.at[CHUNKS + 1]),
        pltpu.make_async_copy(extra_hbm, ext_ref, load_sem.at[CHUNKS + 2]),
    ]
    v_loads = [
        pltpu.make_async_copy(
            basis_hbm.at[pl.ds(k * per, per)], v_ref.at[pl.ds(k * per, per)], load_sem.at[k]
        )
        for k in range(CHUNKS)
    ]
    for copy in v_loads[:1] + loads + v_loads[1:]:
        copy.start()

    barrier = pltpu.get_barrier_semaphore()
    greeted = [up_x, lo_x] + z_peers + xy_peers + core_peers
    for peer in greeted:
        pl.semaphore_signal(barrier, inc=1, device_id=peer, device_id_type=MESH)
    pl.semaphore_wait(barrier, len(greeted))

    sent = []

    def send(src, dst, at, peer):
        copy = pltpu.make_async_remote_copy(
            src, dst, hs_send.at[at], hs_recv.at[at], device_id=peer, device_id_type=MESH
        )
        copy.start()
        sent.append(copy)
        return copy

    low, high = pl.ds(0, HZ), pl.ds(HZ, HZ)
    x_first = [
        send(basis_hbm.at[:, BX - 1, :, low], hxlo.at[:, :, low], 0, up_x),
        send(basis_hbm.at[:, 0, :, high], hxup.at[:, :, high], 1, lo_x),
    ]

    row = lax.broadcasted_iota(jnp.int32, (BY, BZ), 0)
    lane = lax.broadcasted_iota(jnp.int32, (BY, BZ), 1)
    zero = jnp.zeros((BY, BZ), F32)

    for k in range(CHUNKS):
        v_loads[k].wait()
        for i in range(k * per, (k + 1) * per):
            pylo[i] = v_ref[i, :, 0, :]
            pyhi[i] = v_ref[i, :, BY - 1, :]
    y_first = [
        send(pyhi.at[:, :, low], hylo.at[:, :, low], 2, up_y),
        send(pylo.at[:, :, high], hyup.at[:, :, high], 3, lo_y),
    ]
    for copy in loads:
        copy.wait()
    cpack[...] = cf_ref[1, :, BY - 1, :]
    c_sends = [
        send(cf_ref.at[0, BX - 1], cxlo, 4, up_x),
        send(cpack, cylo, 5, up_y),
    ]
    x_later = [
        send(basis_hbm.at[:, BX - 1, :, high], hxlo.at[:, :, high], 6, up_x),
        send(basis_hbm.at[:, 0, :, low], hxup.at[:, :, low], 7, lo_x),
    ]
    y_later = [
        send(pyhi.at[:, :, high], hylo.at[:, :, high], 8, up_y),
        send(pylo.at[:, :, low], hyup.at[:, :, low], 9, lo_y),
    ]

    for x in range(BX):
        cxm[x] = cf_ref[0, x] if x < BX - 1 else jnp.where(last_x, cf_ref[0, x], 0.0)
        cym[x] = jnp.where(jnp.logical_or(row < BY - 1, last_y), cf_ref[1, x], 0.0)

    def local_pair(pair, carry):
        i0 = pair * 2
        base = pl.multiple_of(pair * 16, 16)
        flux_before = [None, None]
        acc = [jnp.zeros((BY, HZ), F32) for _ in range(2)]
        cells = [v_ref[i0 + s, 0] for s in range(2)]
        for x in range(BX):
            outs = []
            nexts = []
            for s in range(2):
                v = cells[s]
                v_up = v_ref[i0 + s, x + 1] if x < BX - 1 else zero
                nexts.append(v_up)
                flux = cxm[x] * (v - v_up)
                out = ext_ref[x] * v + flux
                if x > 0:
                    out = out - flux_before[s]
                flux_before[s] = flux
                v_up = jnp.where(row == BY - 1, 0.0, pltpu.roll(v, BY - 1, 0))
                flux = cym[x] * (v - v_up)
                out = out + flux - jnp.where(row == 0, 0.0, pltpu.roll(flux, 1, 0))
                v_up = jnp.where(lane == BZ - 1, 0.0, pltpu.roll(v, BZ - 1, 1))
                flux = cf_ref[2, x] * (v - v_up)
                out = out + flux - jnp.where(lane == 0, 0.0, pltpu.roll(flux, 1, 1))
                outs.append(out)
                term = v * rhs_ref[x]
                acc[s] = acc[s] + term[:, :HZ] + term[:, HZ:]
            rows, cols = pl.ds(base, 16), pl.ds(x * BZ, BZ)
            vh[rows, cols], vl[rows, cols] = split(jnp.concatenate(cells, axis=0))
            ah[rows, cols], al[rows, cols] = split(jnp.concatenate(outs, axis=0))
            cells = nexts
        for s in range(2):
            proj_acc[i0 + s] = jnp.sum(acc[s], axis=0, keepdims=True)
        return carry

    lax.fori_loop(0, NV // 2, local_pair, 0)
    prod[...] = dot_t(vh[...], ah[...]) + dot_t(vh[...], al[...]) + dot_t(vl[...], ah[...])

    for copy in x_first + y_first + c_sends:
        copy.wait_recv()
    cxlo_v = jnp.where(first_x, 0.0, cxlo[...])
    cylo_v = jnp.where(first_y, 0.0, cylo[...])
    cx_face = jnp.concatenate(
        [cxlo_v[:, :HZ], jnp.where(last_x, 0.0, cf_ref[0, BX - 1, :, HZ:])], axis=1
    )
    cy_face = jnp.concatenate([cylo_v[:, :HZ], jnp.where(last_y, 0.0, cpack[:, HZ:])], axis=1)
    for pair in range(NV // 2):
        for at, coef in ((0, cx_face), (1, cy_face)):
            diffs = []
            flows = []
            for i in (2 * pair, 2 * pair + 1):
                if at == 0:
                    a = v_ref[i, 0, :, :HZ] - hxlo[i, :, :HZ]
                    b = v_ref[i, BX - 1, :, HZ:] - hxup[i, :, HZ:]
                else:
                    a = pylo[i, :, :HZ] - hylo[i, :, :HZ]
                    b = pyhi[i, :, HZ:] - hyup[i, :, HZ:]
                diff = jnp.concatenate([a, b], axis=1)
                diffs.append(diff)
                flows.append(diff * coef)
            rows, cols = pl.ds(16 * pair, 16), pl.ds(at * BZ, BZ)
            fh[rows, cols], fl[rows, cols] = split(jnp.concatenate(diffs, axis=0))
            gh[rows, cols], gl[rows, cols] = split(jnp.concatenate(flows, axis=0))
    total = (
        prod[...] + dot_t(fh[...], gh[...]) + dot_t(fh[...], gl[...]) + dot_t(fl[...], gh[...])
    )
    same = (
        lax.broadcasted_iota(jnp.int32, (NV * BY, NV * BY), 0) % BY
        == lax.broadcasted_iota(jnp.int32, (NV * BY, NV * BY), 1) % BY
    )
    total = jnp.where(same, total, 0.0)
    sums = jnp.sum(total.reshape(NV, BY, NV * BY), axis=1)
    wide = jnp.concatenate([sums[8 * k : 8 * k + 8] for k in range(4)], axis=1)
    s_row = lax.broadcasted_iota(jnp.int32, (4 * NV * BY, 128), 0)
    s_col = lax.broadcasted_iota(jnp.int32, (4 * NV * BY, 128), 1)
    pick = (s_row // BY == s_col).astype(F32)
    packed = jnp.dot(wide, pick, precision=lax.Precision.HIGHEST, preferred_element_type=F32)

    eye_r = lax.broadcasted_iota(jnp.int32, (NV, 128), 0)
    eye_l = lax.broadcasted_iota(jnp.int32, (NV, 128), 1)

    def to_row(col, at):
        return jnp.sum(jnp.where(eye_l == eye_r + at, col, 0.0), axis=0, keepdims=True)

    def to_col(line, at):
        return jnp.sum(jnp.where(eye_l == eye_r + at, line, 0.0), axis=1, keepdims=True)

    proj_col = jnp.sum(proj_acc[...].reshape(NV, HZ), axis=1, keepdims=True)

    ar_waits = []

    def stage(value, src, buf, at, me, peers, count):
        src[...] = value
        for peer in peers:
            pltpu.make_async_remote_copy(
                src, buf.at[me], ar_send.at[at], ar_recv.at[at], device_id=peer, device_id_type=MESH
            ).start()
        buf[me] = value
        others = buf.at[pl.ds(0, count - 1)]
        pltpu.make_async_copy(others, others, ar_recv.at[at]).wait()
        ar_waits.append((others, at))
        return jnp.sum(buf[...], axis=0)

    value = jnp.concatenate([packed, to_row(proj_col, 0)], axis=0)
    value = stage(value, src1.at[0], a1c, 0, core, core_peers, 2)
    value = stage(value, src1.at[1], a1x, 1, xy, xy_peers, n_xy)
    value = stage(value, src1.at[2], a1z, 2, iy, z_peers, n_gy)

    gram = jnp.concatenate(
        [value[0:8]] + [pltpu.roll(value[0:8], 128 - 32 * k, 1) for k in range(1, 4)], axis=0
    )
    gram = jnp.where(eye_l < NV, gram, 0.0)
    proj = to_col(value[8:9], 0)
    mat = jnp.where(eye_l == eye_r + NV, 1.0, jnp.where(eye_l == 2 * NV, proj, gram))
    for k in range(NV):
        col = jnp.broadcast_to(mat[:, k : k + 1], (NV, 128))
        pivot = mat[k : k + 1] / col[k : k + 1]
        mat = jnp.where(eye_r == k, pivot, mat - col * pivot)
    weights = mat[:, 2 * NV : 2 * NV + 1]
    inverse = jnp.where(jnp.logical_and(eye_l >= NV, eye_l < 2 * NV), mat, 0.0)
    wb[...] = jnp.broadcast_to(weights, (NV, 128))

    for copy in x_later + y_later:
        copy.wait_recv()

    def scale(i):
        line = wb[i : i + 1, :]
        return jnp.concatenate([line, line], axis=1)

    guess = [zero for _ in range(BX)]
    halo = [zero for _ in range(4)]
    for i in range(NV):
        w = scale(i)
        for x in range(BX):
            guess[x] = guess[x] + w * v_ref[i, x]
        for at, ref in enumerate((hxlo, hxup, hylo, hyup)):
            halo[at] = halo[at] + w * ref[i]

    def apply(cells, hx_lo, hx_up, hy_lo, hy_up):
        hx_up = jnp.where(last_x, 0.0, hx_up)
        hy_up = jnp.where(last_y, 0.0, hy_up)
        before = cxlo_v * (hx_lo - cells[0])
        outs = []
        for x in range(BX):
            v = cells[x]
            flux = cf_ref[0, x] * (v - (cells[x + 1] if x < BX - 1 else hx_up))
            out = ext_ref[x] * v + flux - before
            before = flux
            v_up = jnp.where(row == BY - 1, hy_up[x : x + 1], pltpu.roll(v, BY - 1, 0))
            flux = cf_ref[1, x] * (v - v_up)
            below = cylo_v[x : x + 1] * (hy_lo[x : x + 1] - v)
            out = out + flux - jnp.where(row == 0, below, pltpu.roll(flux, 1, 0))
            v_up = jnp.where(lane == BZ - 1, 0.0, pltpu.roll(v, BZ - 1, 1))
            flux = cf_ref[2, x] * (v - v_up)
            out = out + flux - jnp.where(lane == 0, 0.0, pltpu.roll(flux, 1, 1))
            outs.append(out)
        return outs

    applied = apply(guess, *halo)
    rd = zero
    for x in range(BX):
        below = cxlo_v if x == 0 else cf_ref[0, x - 1]
        diagonal = ext_ref[x] + cf_ref[0, x] + cf_ref[1, x] + cf_ref[2, x] + below
        diagonal = diagonal + jnp.where(row == 0, cylo_v[x : x + 1], pltpu.roll(cf_ref[1, x], 1, 0))
        diagonal = diagonal + jnp.where(lane == 0, 0.0, pltpu.roll(cf_ref[2, x], 1, 1))
        res = rhs_ref[x] - applied[x]
        cell = res / diagonal
        d_ref[x] = cell
        rd = rd + res * cell
        g_ref[x] = guess[x]
    dplo[...] = d_ref[:, 0, :]
    dphi[...] = d_ref[:, BY - 1, :]
    d_sends = [
        send(d_ref.at[BX - 1], dxlo, 10, up_x),
        send(d_ref.at[0], dxup, 11, lo_x),
        send(dphi, dylo, 12, up_y),
        send(dplo, dyup, 13, lo_y),
    ]
    guess_out = pltpu.make_async_copy(g_ref, guess_hbm, out_sem.at[0])
    guess_out.start()
    w_row = to_row(weights, 0)
    rest = proj - jnp.sum(gram * w_row, axis=1, keepdims=True)
    for copy in d_sends:
        copy.wait_recv()

    cells = [d_ref[x] for x in range(BX)]
    applied = apply(cells, dxlo[...], dxup[...], dylo[...], dyup[...])
    dad = zero
    for x in range(BX):
        dad = dad + cells[x] * applied[x]

    def fold(block):
        return jnp.sum(block[:, :HZ] + block[:, HZ:], axis=0, keepdims=True)

    for i in range(NV):
        acc = v_ref[i, 0] * applied[0]
        for x in range(1, BX):
            acc = acc + v_ref[i, x] * applied[x]
        proj_acc[i] = fold(acc)
    corr_col = jnp.sum(proj_acc[...].reshape(NV, HZ), axis=1, keepdims=True)
    line_at = lax.broadcasted_iota(jnp.int32, (1, 128), 1)
    value = to_row(corr_col, NV)
    value = jnp.where(line_at == 0, jnp.sum(fold(rd), axis=1, keepdims=True), value)
    value = jnp.where(line_at == 1, jnp.sum(fold(dad), axis=1, keepdims=True), value)
    value = stage(value, src2.at[0], a2c, 3, core, core_peers, 2)
    value = stage(value, src2.at[1], a2x, 4, xy, xy_peers, n_xy)
    value = stage(value, src2.at[2], a2z, 5, iy, z_peers, n_gy)

    shift = jnp.sum(inverse * value, axis=1, keepdims=True)
    wb[...] = jnp.broadcast_to(shift, (NV, 128))
    corr = to_col(value, NV)
    numerator = value[:, 0:1] - jnp.sum(shift * rest, axis=0, keepdims=True)
    denominator = value[:, 1:2] - jnp.sum(shift * corr, axis=0, keepdims=True)
    step = numerator / denominator
    update = [d_ref[x] for x in range(BX)]
    for i in range(NV):
        m = scale(i)
        for x in range(BX):
            update[x] = update[x] - m * v_ref[i, x]
    guess_out.wait()
    for x in range(BX):
        o_ref[x] = g_ref[x] + step * update[x]
    stepped_out = pltpu.make_async_copy(o_ref, stepped_hbm, out_sem.at[1])
    stepped_out.start()
    for copy in sent:
        copy.wait_send()
    for others, at in ar_waits:
        pltpu.make_async_copy(others, others, ar_send.at[at]).wait()
    stepped_out.wait()


def solution(mesh):
    n_gx, n_gy = mesh.shape["gx"], mesh.shape["gy"]
    n_xy = n_gx // 2

    def on_device(basis, rhs, extra_diag, coeff):
        vm = pltpu.VMEM
        cell = (BX, BY, BZ)
        slab = (NV, 8, BZ)
        flat = (NV * BY, BX * BZ)
        face = (NV * BY, 2 * BZ)
        anywhere = pl.BlockSpec(memory_space=pl.ANY)
        return pl.pallas_call(
            functools.partial(kernel, n_gx, n_gy),
            out_shape=[jax.ShapeDtypeStruct(cell, F32)] * 2,
            in_specs=[anywhere] * 4,
            out_specs=[anywhere] * 2,
            scratch_shapes=[
                vm((NV,) + cell, F32),
                vm(cell, F32),
                vm(cell, F32),
                vm((3,) + cell, F32),
            ]
            + [vm(flat, BF16)] * 4
            + [vm(face, BF16)] * 4
            + [vm(slab, F32)] * 6
            + [vm(cell, F32)] * 2
            + [vm((8, BZ), F32)] * 3
            + [
                vm((NV, 1, HZ), F32),
                vm((NV * BY, NV * BY), F32),
                vm((NV, 128), F32),
                vm(cell, F32),
                vm(cell, F32),
                vm(cell, F32),
            ]
            + [vm((8, BZ), F32)] * 6
            + [
                vm((3, ROWS, 128), F32),
                vm((3, 1, 128), F32),
                vm((2, ROWS, 128), F32),
                vm((n_xy, ROWS, 128), F32),
                vm((n_gy, ROWS, 128), F32),
                vm((2, 1, 128), F32),
                vm((n_xy, 1, 128), F32),
                vm((n_gy, 1, 128), F32),
                pltpu.SemaphoreType.DMA((CHUNKS + 3,)),
                pltpu.SemaphoreType.DMA((2,)),
                pltpu.SemaphoreType.DMA((14,)),
                pltpu.SemaphoreType.DMA((14,)),
                pltpu.SemaphoreType.DMA((6,)),
                pltpu.SemaphoreType.DMA((6,)),
            ],
            compiler_params=pltpu.CompilerParams(
                collective_id=0, has_side_effects=True, vmem_limit_bytes=48 << 20
            ),
        )(basis, rhs, extra_diag, coeff)

    placed = (
        P(None, "gx", "gy", None),
        P("gx", "gy", None),
        P("gx", "gy", None),
        P(None, "gx", "gy", None),
    )
    return jax.shard_map(
        on_device,
        mesh=mesh,
        in_specs=placed,
        out_specs=(P("gx", "gy", None), P("gx", "gy", None)),
        check_vma=False,
    )
```

```python
import functools

import jax
import jax.numpy as jnp
from jax import lax
from jax.experimental import pallas as pl
from jax.experimental.pallas import tpu as pltpu
from jax.sharding import PartitionSpec as P

MESH = pl.DeviceIdType.MESH
F32 = jnp.float32
BF16 = jnp.bfloat16
NV = 32
BX = 8
BY = 8
BZ = 256
HZ = 128
CHUNKS = 4
ROWS = 9
SIDE = 4


def split(value):
    high = value.astype(BF16)
    low = (value - high.astype(F32)).astype(BF16)
    return high, low


def dot_t(a, b):
    return lax.dot_general(a, b, (((1,), (1,)), ((), ())), preferred_element_type=F32)


def kernel(
    n_gx,
    n_gy,
    basis_hbm,
    rhs_hbm,
    extra_hbm,
    coeff_hbm,
    guess_hbm,
    stepped_hbm,
    v_ref,
    rhs_ref,
    ext_ref,
    cf_ref,
    vh,
    vl,
    ah,
    al,
    fh,
    fl,
    gh,
    gl,
    pylo,
    pyhi,
    hxlo,
    hxup,
    hylo,
    hyup,
    cxm,
    cym,
    cpack,
    cxlo,
    cylo,
    proj_acc,
    prod,
    wb,
    g_ref,
    d_ref,
    o_ref,
    dplo,
    dphi,
    dxlo,
    dxup,
    dylo,
    dyup,
    src1,
    src2,
    a1c,
    a1x,
    a1z,
    a2c,
    a2x,
    a2z,
    load_sem,
    out_sem,
    hs_send,
    hs_recv,
    ar_send,
    ar_recv,
    news,
):
    ix = lax.axis_index("gx")
    iy = lax.axis_index("gy")
    core = ix % 2
    xy = ix // 2
    n_xy = n_gx // 2
    side = SIDE
    up_x = ((ix + 1) % n_gx, iy)
    lo_x = ((ix + n_gx - 1) % n_gx, iy)
    up_y = (ix, (iy + 1) % n_gy)
    lo_y = (ix, (iy + n_gy - 1) % n_gy)
    x_at, y_at = xy % side, xy // side
    row_peers = [((y_at * side + (x_at + t) % side) * 2 + core, iy) for t in range(1, side)]
    column_peers = [
        (((y_at + t) % (n_xy // side) * side + x_at) * 2 + core, iy) for t in range(1, n_xy // side)
    ]
    z_at = {t: (ix, (iy + n_gy + t) % n_gy) for t in (-4, -2, -1, 1, 2, 4)}
    core_peers = [(xy * 2 + (core + 1) % 2, iy)]
    xy_peers = [(((xy + t) % n_xy) * 2 + core, iy) for t in range(1, n_xy)]
    z_peers = [(ix, (iy + t) % n_gy) for t in range(1, n_gy)]
    first_x, last_x = ix == 0, ix == n_gx - 1
    first_y, last_y = iy == 0, iy == n_gy - 1

    per = NV // CHUNKS
    loads = [
        pltpu.make_async_copy(coeff_hbm, cf_ref, load_sem.at[CHUNKS]),
        pltpu.make_async_copy(rhs_hbm, rhs_ref, load_sem.at[CHUNKS + 1]),
        pltpu.make_async_copy(extra_hbm, ext_ref, load_sem.at[CHUNKS + 2]),
    ]
    v_loads = [
        pltpu.make_async_copy(
            basis_hbm.at[pl.ds(k * per, per)], v_ref.at[pl.ds(k * per, per)], load_sem.at[k]
        )
        for k in range(CHUNKS)
    ]
    for copy in v_loads[:1] + loads + v_loads[1:]:
        copy.start()

    barrier = pltpu.get_barrier_semaphore()
    greeted = [up_x, lo_x] + [z_at[t] for t in (1, -1, 2, -2)]
    greeted = greeted + row_peers + column_peers + core_peers
    for peer in greeted:
        pl.semaphore_signal(barrier, inc=1, device_id=peer, device_id_type=MESH)

    row = lax.broadcasted_iota(jnp.int32, (BY, BZ), 0)
    lane = lax.broadcasted_iota(jnp.int32, (BY, BZ), 1)
    zero = jnp.zeros((BY, BZ), F32)

    for k in range(CHUNKS):
        v_loads[k].wait()
        for i in range(k * per, (k + 1) * per):
            pylo[i] = v_ref[i, :, 0, :]
            pyhi[i] = v_ref[i, :, BY - 1, :]
    for copy in loads:
        copy.wait()
    cpack[...] = cf_ref[1, :, BY - 1, :]
    pl.semaphore_wait(barrier, len(greeted))

    def tell(peers, at):
        for peer in peers:
            pl.semaphore_signal(news.at[at], inc=1, device_id=peer, device_id_type=MESH)

    sent = []

    def send(src, dst, at, peer):
        copy = pltpu.make_async_remote_copy(
            src, dst, hs_send.at[at], hs_recv.at[at], device_id=peer, device_id_type=MESH
        )
        copy.start()
        sent.append(copy)
        return copy

    low, high = pl.ds(0, HZ), pl.ds(HZ, HZ)
    y_first = [
        send(pyhi.at[:, :, low], hylo.at[:, :, low], 2, up_y),
        send(pylo.at[:, :, high], hyup.at[:, :, high], 3, lo_y),
    ]
    x_first = [
        send(basis_hbm.at[:, BX - 1, :, low], hxlo.at[:, :, low], 0, up_x),
        send(basis_hbm.at[:, 0, :, high], hxup.at[:, :, high], 1, lo_x),
    ]

    c_sends = [
        send(cf_ref.at[0, BX - 1], cxlo, 4, up_x),
        send(cpack, cylo, 5, up_y),
    ]
    tell(row_peers, 0)
    tell([z_at[2], z_at[-2]], 1)
    x_later = [
        send(basis_hbm.at[:, BX - 1, :, high], hxlo.at[:, :, high], 6, up_x),
        send(basis_hbm.at[:, 0, :, low], hxup.at[:, :, low], 7, lo_x),
    ]
    y_later = [
        send(pyhi.at[:, :, high], hylo.at[:, :, high], 8, up_y),
        send(pylo.at[:, :, low], hyup.at[:, :, low], 9, lo_y),
    ]

    for x in range(BX):
        cxm[x] = cf_ref[0, x] if x < BX - 1 else jnp.where(last_x, cf_ref[0, x], 0.0)
        cym[x] = jnp.where(jnp.logical_or(row < BY - 1, last_y), cf_ref[1, x], 0.0)

    def local_pair(pair, carry):
        i0 = pair * 2
        base = pl.multiple_of(pair * 16, 16)
        flux_before = [None, None]
        acc = [jnp.zeros((BY, HZ), F32) for _ in range(2)]
        cells = [v_ref[i0 + s, 0] for s in range(2)]
        for x in range(BX):
            outs = []
            nexts = []
            for s in range(2):
                v = cells[s]
                v_up = v_ref[i0 + s, x + 1] if x < BX - 1 else zero
                nexts.append(v_up)
                flux = cxm[x] * (v - v_up)
                out = ext_ref[x] * v + flux
                if x > 0:
                    out = out - flux_before[s]
                flux_before[s] = flux
                v_up = jnp.where(row == BY - 1, 0.0, pltpu.roll(v, BY - 1, 0))
                flux = cym[x] * (v - v_up)
                out = out + flux - jnp.where(row == 0, 0.0, pltpu.roll(flux, 1, 0))
                v_up = jnp.where(lane == BZ - 1, 0.0, pltpu.roll(v, BZ - 1, 1))
                flux = cf_ref[2, x] * (v - v_up)
                out = out + flux - jnp.where(lane == 0, 0.0, pltpu.roll(flux, 1, 1))
                outs.append(out)
                term = v * rhs_ref[x]
                acc[s] = acc[s] + term[:, :HZ] + term[:, HZ:]
            rows, cols = pl.ds(base, 16), pl.ds(x * BZ, BZ)
            vh[rows, cols], vl[rows, cols] = split(jnp.concatenate(cells, axis=0))
            ah[rows, cols], al[rows, cols] = split(jnp.concatenate(outs, axis=0))
            cells = nexts
        for s in range(2):
            proj_acc[i0 + s] = jnp.sum(acc[s], axis=0, keepdims=True)
        return carry

    lax.fori_loop(0, NV // 2, local_pair, 0)
    pl.semaphore_wait(news.at[0], len(row_peers))
    pl.semaphore_wait(news.at[1], 2)
    tell([z_at[4], z_at[-4]], 2)
    prod[...] = dot_t(vh[...], ah[...]) + dot_t(vh[...], al[...]) + dot_t(vl[...], ah[...])

    for copy in x_first + y_first + c_sends:
        copy.wait_recv()
    cxlo_v = jnp.where(first_x, 0.0, cxlo[...])
    cylo_v = jnp.where(first_y, 0.0, cylo[...])
    cx_face = jnp.concatenate(
        [cxlo_v[:, :HZ], jnp.where(last_x, 0.0, cf_ref[0, BX - 1, :, HZ:])], axis=1
    )
    cy_face = jnp.concatenate([cylo_v[:, :HZ], jnp.where(last_y, 0.0, cpack[:, HZ:])], axis=1)
    for pair in range(NV // 2):
        for at, coef in ((0, cx_face), (1, cy_face)):
            diffs = []
            flows = []
            for i in (2 * pair, 2 * pair + 1):
                if at == 0:
                    a = v_ref[i, 0, :, :HZ] - hxlo[i, :, :HZ]
                    b = v_ref[i, BX - 1, :, HZ:] - hxup[i, :, HZ:]
                else:
                    a = pylo[i, :, :HZ] - hylo[i, :, :HZ]
                    b = pyhi[i, :, HZ:] - hyup[i, :, HZ:]
                diff = jnp.concatenate([a, b], axis=1)
                diffs.append(diff)
                flows.append(diff * coef)
            rows, cols = pl.ds(16 * pair, 16), pl.ds(at * BZ, BZ)
            fh[rows, cols], fl[rows, cols] = split(jnp.concatenate(diffs, axis=0))
            gh[rows, cols], gl[rows, cols] = split(jnp.concatenate(flows, axis=0))
    total = (
        prod[...] + dot_t(fh[...], gh[...]) + dot_t(fh[...], gl[...]) + dot_t(fl[...], gh[...])
    )
    same = (
        lax.broadcasted_iota(jnp.int32, (NV * BY, NV * BY), 0) % BY
        == lax.broadcasted_iota(jnp.int32, (NV * BY, NV * BY), 1) % BY
    )
    total = jnp.where(same, total, 0.0)
    sums = jnp.sum(total.reshape(NV, BY, NV * BY), axis=1)
    wide = jnp.concatenate([sums[8 * k : 8 * k + 8] for k in range(4)], axis=1)
    s_row = lax.broadcasted_iota(jnp.int32, (4 * NV * BY, 128), 0)
    s_col = lax.broadcasted_iota(jnp.int32, (4 * NV * BY, 128), 1)
    pick = (s_row // BY == s_col).astype(F32)
    packed = jnp.dot(wide, pick, precision=lax.Precision.HIGHEST, preferred_element_type=F32)

    eye_r = lax.broadcasted_iota(jnp.int32, (NV, 128), 0)
    eye_l = lax.broadcasted_iota(jnp.int32, (NV, 128), 1)

    def to_row(col, at):
        return jnp.sum(jnp.where(eye_l == eye_r + at, col, 0.0), axis=0, keepdims=True)

    def to_col(line, at):
        return jnp.sum(jnp.where(eye_l == eye_r + at, line, 0.0), axis=1, keepdims=True)

    proj_col = jnp.sum(proj_acc[...].reshape(NV, HZ), axis=1, keepdims=True)

    ar_waits = []

    def stage(value, src, buf, at, me, peers, count):
        src[...] = value
        for peer in peers:
            pltpu.make_async_remote_copy(
                src, buf.at[me], ar_send.at[at], ar_recv.at[at], device_id=peer, device_id_type=MESH
            ).start()
        buf[me] = value
        others = buf.at[pl.ds(0, count - 1)]
        pltpu.make_async_copy(others, others, ar_recv.at[at]).wait()
        ar_waits.append((others, at))
        return jnp.sum(buf[...], axis=0)

    value = jnp.concatenate([packed, to_row(proj_col, 0)], axis=0)
    value = stage(value, src1.at[0], a1c, 0, core, core_peers, 2)
    value = stage(value, src1.at[1], a1x, 1, xy, xy_peers, n_xy)
    pl.semaphore_wait(news.at[2], 2)
    value = stage(value, src1.at[2], a1z, 2, iy, z_peers, n_gy)

    gram = jnp.concatenate(
        [value[0:8]] + [pltpu.roll(value[0:8], 128 - 32 * k, 1) for k in range(1, 4)], axis=0
    )
    gram = jnp.where(eye_l < NV, gram, 0.0)
    proj = to_col(value[8:9], 0)
    mat = jnp.where(eye_l == eye_r + NV, 1.0, jnp.where(eye_l == 2 * NV, proj, gram))
    for k in range(NV):
        col = jnp.broadcast_to(mat[:, k : k + 1], (NV, 128))
        pivot = mat[k : k + 1] / col[k : k + 1]
        mat = jnp.where(eye_r == k, pivot, mat - col * pivot)
    weights = mat[:, 2 * NV : 2 * NV + 1]
    inverse = jnp.where(jnp.logical_and(eye_l >= NV, eye_l < 2 * NV), mat, 0.0)
    wb[...] = jnp.broadcast_to(weights, (NV, 128))

    for copy in x_later + y_later:
        copy.wait_recv()

    def scale(i):
        line = wb[i : i + 1, :]
        return jnp.concatenate([line, line], axis=1)

    guess = [zero for _ in range(BX)]
    halo = [zero for _ in range(4)]
    for i in range(NV):
        w = scale(i)
        for x in range(BX):
            guess[x] = guess[x] + w * v_ref[i, x]
        for at, ref in enumerate((hxlo, hxup, hylo, hyup)):
            halo[at] = halo[at] + w * ref[i]

    def apply(cells, hx_lo, hx_up, hy_lo, hy_up):
        hx_up = jnp.where(last_x, 0.0, hx_up)
        hy_up = jnp.where(last_y, 0.0, hy_up)
        before = cxlo_v * (hx_lo - cells[0])
        outs = []
        for x in range(BX):
            v = cells[x]
            flux = cf_ref[0, x] * (v - (cells[x + 1] if x < BX - 1 else hx_up))
            out = ext_ref[x] * v + flux - before
            before = flux
            v_up = jnp.where(row == BY - 1, hy_up[x : x + 1], pltpu.roll(v, BY - 1, 0))
            flux = cf_ref[1, x] * (v - v_up)
            below = cylo_v[x : x + 1] * (hy_lo[x : x + 1] - v)
            out = out + flux - jnp.where(row == 0, below, pltpu.roll(flux, 1, 0))
            v_up = jnp.where(lane == BZ - 1, 0.0, pltpu.roll(v, BZ - 1, 1))
            flux = cf_ref[2, x] * (v - v_up)
            out = out + flux - jnp.where(lane == 0, 0.0, pltpu.roll(flux, 1, 1))
            outs.append(out)
        return outs

    applied = apply(guess, *halo)
    rd = zero
    for x in range(BX):
        below = cxlo_v if x == 0 else cf_ref[0, x - 1]
        diagonal = ext_ref[x] + cf_ref[0, x] + cf_ref[1, x] + cf_ref[2, x] + below
        diagonal = diagonal + jnp.where(row == 0, cylo_v[x : x + 1], pltpu.roll(cf_ref[1, x], 1, 0))
        diagonal = diagonal + jnp.where(lane == 0, 0.0, pltpu.roll(cf_ref[2, x], 1, 1))
        res = rhs_ref[x] - applied[x]
        cell = res / diagonal
        d_ref[x] = cell
        rd = rd + res * cell
        g_ref[x] = guess[x]
    dplo[...] = d_ref[:, 0, :]
    dphi[...] = d_ref[:, BY - 1, :]
    d_sends = [
        send(d_ref.at[BX - 1], dxlo, 10, up_x),
        send(d_ref.at[0], dxup, 11, lo_x),
        send(dphi, dylo, 12, up_y),
        send(dplo, dyup, 13, lo_y),
    ]
    guess_out = pltpu.make_async_copy(g_ref, guess_hbm, out_sem.at[0])
    guess_out.start()
    w_row = to_row(weights, 0)
    rest = proj - jnp.sum(gram * w_row, axis=1, keepdims=True)
    for copy in d_sends:
        copy.wait_recv()

    cells = [d_ref[x] for x in range(BX)]
    applied = apply(cells, dxlo[...], dxup[...], dylo[...], dyup[...])
    dad = zero
    for x in range(BX):
        dad = dad + cells[x] * applied[x]

    def fold(block):
        return jnp.sum(block[:, :HZ] + block[:, HZ:], axis=0, keepdims=True)

    for i in range(NV):
        acc = v_ref[i, 0] * applied[0]
        for x in range(1, BX):
            acc = acc + v_ref[i, x] * applied[x]
        proj_acc[i] = fold(acc)
    corr_col = jnp.sum(proj_acc[...].reshape(NV, HZ), axis=1, keepdims=True)
    line_at = lax.broadcasted_iota(jnp.int32, (1, 128), 1)
    value = to_row(corr_col, NV)
    value = jnp.where(line_at == 0, jnp.sum(fold(rd), axis=1, keepdims=True), value)
    value = jnp.where(line_at == 1, jnp.sum(fold(dad), axis=1, keepdims=True), value)
    value = stage(value, src2.at[0], a2c, 3, core, core_peers, 2)
    value = stage(value, src2.at[1], a2x, 4, xy, xy_peers, n_xy)
    value = stage(value, src2.at[2], a2z, 5, iy, z_peers, n_gy)

    shift = jnp.sum(inverse * value, axis=1, keepdims=True)
    wb[...] = jnp.broadcast_to(shift, (NV, 128))
    corr = to_col(value, NV)
    numerator = value[:, 0:1] - jnp.sum(shift * rest, axis=0, keepdims=True)
    denominator = value[:, 1:2] - jnp.sum(shift * corr, axis=0, keepdims=True)
    step = numerator / denominator
    update = [d_ref[x] for x in range(BX)]
    for i in range(NV):
        m = scale(i)
        for x in range(BX):
            update[x] = update[x] - m * v_ref[i, x]
    guess_out.wait()
    for x in range(BX):
        o_ref[x] = g_ref[x] + step * update[x]
    stepped_out = pltpu.make_async_copy(o_ref, stepped_hbm, out_sem.at[1])
    stepped_out.start()
    for copy in sent:
        copy.wait_send()
    for others, at in ar_waits:
        pltpu.make_async_copy(others, others, ar_send.at[at]).wait()
    stepped_out.wait()


def solution(mesh):
    n_gx, n_gy = mesh.shape["gx"], mesh.shape["gy"]
    n_xy = n_gx // 2

    def on_device(basis, rhs, extra_diag, coeff):
        vm = pltpu.VMEM
        cell = (BX, BY, BZ)
        slab = (NV, 8, BZ)
        flat = (NV * BY, BX * BZ)
        face = (NV * BY, 2 * BZ)
        anywhere = pl.BlockSpec(memory_space=pl.ANY)
        return pl.pallas_call(
            functools.partial(kernel, n_gx, n_gy),
            out_shape=[jax.ShapeDtypeStruct(cell, F32)] * 2,
            in_specs=[anywhere] * 4,
            out_specs=[anywhere] * 2,
            scratch_shapes=[
                vm((NV,) + cell, F32),
                vm(cell, F32),
                vm(cell, F32),
                vm((3,) + cell, F32),
            ]
            + [vm(flat, BF16)] * 4
            + [vm(face, BF16)] * 4
            + [vm(slab, F32)] * 6
            + [vm(cell, F32)] * 2
            + [vm((8, BZ), F32)] * 3
            + [
                vm((NV, 1, HZ), F32),
                vm((NV * BY, NV * BY), F32),
                vm((NV, 128), F32),
                vm(cell, F32),
                vm(cell, F32),
                vm(cell, F32),
            ]
            + [vm((8, BZ), F32)] * 6
            + [
                vm((3, ROWS, 128), F32),
                vm((3, 1, 128), F32),
                vm((2, ROWS, 128), F32),
                vm((n_xy, ROWS, 128), F32),
                vm((n_gy, ROWS, 128), F32),
                vm((2, 1, 128), F32),
                vm((n_xy, 1, 128), F32),
                vm((n_gy, 1, 128), F32),
                pltpu.SemaphoreType.DMA((CHUNKS + 3,)),
                pltpu.SemaphoreType.DMA((2,)),
                pltpu.SemaphoreType.DMA((14,)),
                pltpu.SemaphoreType.DMA((14,)),
                pltpu.SemaphoreType.DMA((6,)),
                pltpu.SemaphoreType.DMA((6,)),
                pltpu.SemaphoreType.REGULAR((3,)),
            ],
            compiler_params=pltpu.CompilerParams(
                collective_id=0, has_side_effects=True, vmem_limit_bytes=63 << 20
            ),
        )(basis, rhs, extra_diag, coeff)

    placed = (
        P(None, "gx", "gy", None),
        P("gx", "gy", None),
        P("gx", "gy", None),
        P(None, "gx", "gy", None),
    )
    return jax.shard_map(
        on_device,
        mesh=mesh,
        in_specs=placed,
        out_specs=(P("gx", "gy", None), P("gx", "gy", None)),
        check_vma=False,
    )
```

```python
import functools

import jax
import jax.numpy as jnp
from jax import lax
from jax.experimental import pallas as pl
from jax.experimental.pallas import tpu as pltpu
from jax.sharding import PartitionSpec as P

MESH = pl.DeviceIdType.MESH
F32 = jnp.float32
BF16 = jnp.bfloat16
NV = 32
BX = 8
BY = 8
BZ = 256
HZ = 128
CHUNKS = 4
ROWS = 9
SIDE = 4
PIVOTS = 4
EARLY = 4


def split(value):
    high = value.astype(BF16)
    low = (value - high.astype(F32)).astype(BF16)
    return high, low


def dot_t(a, b):
    return lax.dot_general(a, b, (((1,), (1,)), ((), ())), preferred_element_type=F32)


def kernel(
    n_gx,
    n_gy,
    basis_hbm,
    rhs_hbm,
    extra_hbm,
    coeff_hbm,
    g_ref,
    o_ref,
    v_ref,
    rhs_ref,
    ext_ref,
    cf_ref,
    vh,
    vl,
    ah,
    al,
    fh,
    fl,
    gh,
    gl,
    pylo,
    pyhi,
    hxlo,
    hxup,
    hylo,
    hyup,
    cxm,
    cym,
    cpack,
    cxlo,
    cylo,
    proj_acc,
    prod,
    wb,
    d_ref,
    dplo,
    dphi,
    dxlo,
    dxup,
    dylo,
    dyup,
    src1,
    src2,
    a1c,
    a1x,
    a1z,
    a2c,
    a2x,
    a2z,
    load_sem,
    hs_send,
    hs_recv,
    ar_send,
    ar_recv,
    news,
):
    ix = lax.axis_index("gx")
    iy = lax.axis_index("gy")
    core = ix % 2
    xy = ix // 2
    n_xy = n_gx // 2
    side = SIDE
    up_x = ((ix + 1) % n_gx, iy)
    lo_x = ((ix + n_gx - 1) % n_gx, iy)
    up_y = (ix, (iy + 1) % n_gy)
    lo_y = (ix, (iy + n_gy - 1) % n_gy)
    x_at, y_at = xy % side, xy // side
    row_peers = [((y_at * side + (x_at + t) % side) * 2 + core, iy) for t in range(1, side)]
    column_peers = [
        (((y_at + t) % (n_xy // side) * side + x_at) * 2 + core, iy) for t in range(1, n_xy // side)
    ]
    z_at = {t: (ix, (iy + n_gy + t) % n_gy) for t in (-4, -2, -1, 1, 2, 4)}
    core_peers = [(xy * 2 + (core + 1) % 2, iy)]
    xy_peers = [(((xy + t) % n_xy) * 2 + core, iy) for t in range(1, n_xy)]
    z_peers = [(ix, (iy + t) % n_gy) for t in range(1, n_gy)]
    first_x, last_x = ix == 0, ix == n_gx - 1
    first_y, last_y = iy == 0, iy == n_gy - 1

    per = NV // CHUNKS
    loads = [
        pltpu.make_async_copy(coeff_hbm, cf_ref, load_sem.at[CHUNKS]),
        pltpu.make_async_copy(rhs_hbm, rhs_ref, load_sem.at[CHUNKS + 1]),
        pltpu.make_async_copy(extra_hbm, ext_ref, load_sem.at[CHUNKS + 2]),
    ]
    v_loads = [
        pltpu.make_async_copy(
            basis_hbm.at[pl.ds(k * per, per)], v_ref.at[pl.ds(k * per, per)], load_sem.at[k]
        )
        for k in range(CHUNKS)
    ]
    for copy in v_loads[:1] + loads + v_loads[1:]:
        copy.start()

    barrier = pltpu.get_barrier_semaphore()
    greeted = [up_x, lo_x] + [z_at[t] for t in (1, -1, 2, -2)]
    greeted = greeted + row_peers + column_peers + core_peers
    for peer in greeted:
        pl.semaphore_signal(barrier, inc=1, device_id=peer, device_id_type=MESH)

    row = lax.broadcasted_iota(jnp.int32, (BY, BZ), 0)
    lane = lax.broadcasted_iota(jnp.int32, (BY, BZ), 1)
    zero = jnp.zeros((BY, BZ), F32)

    def coefficient_masks():
        for x in range(BX):
            cxm[x] = cf_ref[0, x] if x < BX - 1 else jnp.where(last_x, cf_ref[0, x], 0.0)
            cym[x] = jnp.where(jnp.logical_or(row < BY - 1, last_y), cf_ref[1, x], 0.0)

    def local_pair(pair, carry):
        i0 = pair * 2
        base = pl.multiple_of(pair * 16, 16)
        flux_before = [None, None]
        acc = [jnp.zeros((BY, HZ), F32) for _ in range(2)]
        cells = [v_ref[i0 + s, 0] for s in range(2)]
        for x in range(BX):
            outs = []
            nexts = []
            for s in range(2):
                v = cells[s]
                v_up = v_ref[i0 + s, x + 1] if x < BX - 1 else zero
                nexts.append(v_up)
                flux = cxm[x] * (v - v_up)
                out = ext_ref[x] * v + flux
                if x > 0:
                    out = out - flux_before[s]
                flux_before[s] = flux
                v_up = jnp.where(row == BY - 1, 0.0, pltpu.roll(v, BY - 1, 0))
                flux = cym[x] * (v - v_up)
                out = out + flux - jnp.where(row == 0, 0.0, pltpu.roll(flux, 1, 0))
                v_up = jnp.where(lane == BZ - 1, 0.0, pltpu.roll(v, BZ - 1, 1))
                flux = cf_ref[2, x] * (v - v_up)
                out = out + flux - jnp.where(lane == 0, 0.0, pltpu.roll(flux, 1, 1))
                outs.append(out)
                term = v * rhs_ref[x]
                acc[s] = acc[s] + term[:, :HZ] + term[:, HZ:]
            rows, cols = pl.ds(base, 16), pl.ds(x * BZ, BZ)
            vh[rows, cols], vl[rows, cols] = split(jnp.concatenate(cells, axis=0))
            ah[rows, cols], al[rows, cols] = split(jnp.concatenate(outs, axis=0))
            cells = nexts
        for s in range(2):
            proj_acc[i0 + s] = jnp.sum(acc[s], axis=0, keepdims=True)
        return carry

    for k in range(CHUNKS):
        v_loads[k].wait()
        for i in range(k * per, (k + 1) * per):
            pylo[i] = v_ref[i, :, 0, :]
            pyhi[i] = v_ref[i, :, BY - 1, :]
    for copy in loads:
        copy.wait()
    cpack[...] = cf_ref[1, :, BY - 1, :]
    coefficient_masks()
    lax.fori_loop(0, EARLY, local_pair, 0)
    pl.semaphore_wait(barrier, len(greeted))

    def tell(peers, at):
        for peer in peers:
            pl.semaphore_signal(news.at[at], inc=1, device_id=peer, device_id_type=MESH)

    sent = []

    def send(src, dst, at, peer):
        copy = pltpu.make_async_remote_copy(
            src, dst, hs_send.at[at], hs_recv.at[at], device_id=peer, device_id_type=MESH
        )
        copy.start()
        sent.append(copy)
        return copy

    low, high = pl.ds(0, HZ), pl.ds(HZ, HZ)
    y_first = [
        send(pyhi.at[:, :, low], hylo.at[:, :, low], 2, up_y),
        send(pylo.at[:, :, high], hyup.at[:, :, high], 3, lo_y),
    ]
    x_first = [
        send(basis_hbm.at[:, BX - 1, :, low], hxlo.at[:, :, low], 0, up_x),
        send(basis_hbm.at[:, 0, :, high], hxup.at[:, :, high], 1, lo_x),
    ]

    c_sends = [
        send(cf_ref.at[0, BX - 1], cxlo, 4, up_x),
        send(cpack, cylo, 5, up_y),
    ]
    tell(row_peers, 0)
    tell([z_at[2], z_at[-2]], 1)
    x_later = [
        send(basis_hbm.at[:, BX - 1, :, high], hxlo.at[:, :, high], 6, up_x),
        send(basis_hbm.at[:, 0, :, low], hxup.at[:, :, low], 7, lo_x),
    ]
    y_later = [
        send(pyhi.at[:, :, high], hylo.at[:, :, high], 8, up_y),
        send(pylo.at[:, :, low], hyup.at[:, :, low], 9, lo_y),
    ]

    lax.fori_loop(EARLY, NV // 2, local_pair, 0)
    pl.semaphore_wait(news.at[0], len(row_peers))
    pl.semaphore_wait(news.at[1], 2)
    tell([z_at[4], z_at[-4]], 2)
    prod[...] = dot_t(vh[...], ah[...]) + dot_t(vh[...], al[...]) + dot_t(vl[...], ah[...])

    for copy in x_first + y_first + c_sends:
        copy.wait_recv()
    cxlo_v = jnp.where(first_x, 0.0, cxlo[...])
    cylo_v = jnp.where(first_y, 0.0, cylo[...])
    cx_face = jnp.concatenate(
        [cxlo_v[:, :HZ], jnp.where(last_x, 0.0, cf_ref[0, BX - 1, :, HZ:])], axis=1
    )
    cy_face = jnp.concatenate([cylo_v[:, :HZ], jnp.where(last_y, 0.0, cpack[:, HZ:])], axis=1)
    for pair in range(NV // 2):
        for at, coef in ((0, cx_face), (1, cy_face)):
            diffs = []
            flows = []
            for i in (2 * pair, 2 * pair + 1):
                if at == 0:
                    a = v_ref[i, 0, :, :HZ] - hxlo[i, :, :HZ]
                    b = v_ref[i, BX - 1, :, HZ:] - hxup[i, :, HZ:]
                else:
                    a = pylo[i, :, :HZ] - hylo[i, :, :HZ]
                    b = pyhi[i, :, HZ:] - hyup[i, :, HZ:]
                diff = jnp.concatenate([a, b], axis=1)
                diffs.append(diff)
                flows.append(diff * coef)
            rows, cols = pl.ds(16 * pair, 16), pl.ds(at * BZ, BZ)
            fh[rows, cols], fl[rows, cols] = split(jnp.concatenate(diffs, axis=0))
            gh[rows, cols], gl[rows, cols] = split(jnp.concatenate(flows, axis=0))
    total = (
        prod[...] + dot_t(fh[...], gh[...]) + dot_t(fh[...], gl[...]) + dot_t(fl[...], gh[...])
    )
    same = (
        lax.broadcasted_iota(jnp.int32, (NV * BY, NV * BY), 0) % BY
        == lax.broadcasted_iota(jnp.int32, (NV * BY, NV * BY), 1) % BY
    )
    total = jnp.where(same, total, 0.0)
    sums = jnp.sum(total.reshape(NV, BY, NV * BY), axis=1)
    wide = jnp.concatenate([sums[8 * k : 8 * k + 8] for k in range(4)], axis=1)
    s_row = lax.broadcasted_iota(jnp.int32, (4 * NV * BY, 128), 0)
    s_col = lax.broadcasted_iota(jnp.int32, (4 * NV * BY, 128), 1)
    pick = (s_row // BY == s_col).astype(F32)
    packed = jnp.dot(wide, pick, precision=lax.Precision.HIGHEST, preferred_element_type=F32)

    eye_r = lax.broadcasted_iota(jnp.int32, (NV, 128), 0)
    eye_l = lax.broadcasted_iota(jnp.int32, (NV, 128), 1)

    def to_row(col, at):
        return jnp.sum(jnp.where(eye_l == eye_r + at, col, 0.0), axis=0, keepdims=True)

    def to_col(line, at):
        return jnp.sum(jnp.where(eye_l == eye_r + at, line, 0.0), axis=1, keepdims=True)

    proj_col = jnp.sum(proj_acc[...].reshape(NV, HZ), axis=1, keepdims=True)

    ar_waits = []

    def stage(value, src, buf, at, me, peers, count):
        src[...] = value
        for peer in peers:
            pltpu.make_async_remote_copy(
                src, buf.at[me], ar_send.at[at], ar_recv.at[at], device_id=peer, device_id_type=MESH
            ).start()
        buf[me] = value
        others = buf.at[pl.ds(0, count - 1)]
        pltpu.make_async_copy(others, others, ar_recv.at[at]).wait()
        ar_waits.append((others, at))
        return jnp.sum(buf[...], axis=0)

    value = jnp.concatenate([packed, to_row(proj_col, 0)], axis=0)
    value = stage(value, src1.at[0], a1c, 0, core, core_peers, 2)
    value = stage(value, src1.at[1], a1x, 1, xy, xy_peers, n_xy)
    pl.semaphore_wait(news.at[2], 2)
    value = stage(value, src1.at[2], a1z, 2, iy, z_peers, n_gy)

    gram = jnp.concatenate(
        [value[0:8]] + [pltpu.roll(value[0:8], 128 - 32 * k, 1) for k in range(1, 4)], axis=0
    )
    gram = jnp.where(eye_l < NV, gram, 0.0)
    proj = to_col(value[8:9], 0)
    mat = jnp.where(eye_l == eye_r + NV, 1.0, jnp.where(eye_l == 2 * NV, proj, gram))
    for k in range(0, NV, PIVOTS):
        cols = [jnp.broadcast_to(mat[:, k + j : k + j + 1], (NV, 128)) for j in range(PIVOTS)]
        rows = [mat[k + j : k + j + 1] for j in range(PIVOTS)]
        head = [[cols[j][k + i : k + i + 1] for j in range(PIVOTS)] for i in range(PIVOTS)]
        for j in range(PIVOTS):
            scaled = 1.0 / head[j][j]
            rows[j] = rows[j] * scaled
            for m in range(j + 1, PIVOTS):
                head[j][m] = head[j][m] * scaled
            for i in range(PIVOTS):
                if i != j:
                    rows[i] = rows[i] - head[i][j] * rows[j]
                    for m in range(j + 1, PIVOTS):
                        head[i][m] = head[i][m] - head[i][j] * head[j][m]
        for j in range(PIVOTS):
            mat = mat - cols[j] * rows[j]
        for j in range(PIVOTS):
            mat = jnp.where(eye_r == k + j, rows[j], mat)
    weights = mat[:, 2 * NV : 2 * NV + 1]
    inverse = jnp.where(jnp.logical_and(eye_l >= NV, eye_l < 2 * NV), mat, 0.0)
    wb[...] = jnp.broadcast_to(weights, (NV, 128))

    for copy in x_later + y_later:
        copy.wait_recv()

    def scale(i):
        line = wb[i : i + 1, :]
        return jnp.concatenate([line, line], axis=1)

    guess = [zero for _ in range(BX)]
    halo = [zero for _ in range(4)]
    for i in range(NV):
        w = scale(i)
        for x in range(BX):
            guess[x] = guess[x] + w * v_ref[i, x]
        for at, ref in enumerate((hxlo, hxup, hylo, hyup)):
            halo[at] = halo[at] + w * ref[i]

    def apply(cells, hx_lo, hx_up, hy_lo, hy_up):
        hx_up = jnp.where(last_x, 0.0, hx_up)
        hy_up = jnp.where(last_y, 0.0, hy_up)
        before = cxlo_v * (hx_lo - cells[0])
        outs = []
        for x in range(BX):
            v = cells[x]
            flux = cf_ref[0, x] * (v - (cells[x + 1] if x < BX - 1 else hx_up))
            out = ext_ref[x] * v + flux - before
            before = flux
            v_up = jnp.where(row == BY - 1, hy_up[x : x + 1], pltpu.roll(v, BY - 1, 0))
            flux = cf_ref[1, x] * (v - v_up)
            below = cylo_v[x : x + 1] * (hy_lo[x : x + 1] - v)
            out = out + flux - jnp.where(row == 0, below, pltpu.roll(flux, 1, 0))
            v_up = jnp.where(lane == BZ - 1, 0.0, pltpu.roll(v, BZ - 1, 1))
            flux = cf_ref[2, x] * (v - v_up)
            out = out + flux - jnp.where(lane == 0, 0.0, pltpu.roll(flux, 1, 1))
            outs.append(out)
        return outs

    applied = apply(guess, *halo)
    rd = zero
    for x in range(BX):
        below = cxlo_v if x == 0 else cf_ref[0, x - 1]
        diagonal = ext_ref[x] + cf_ref[0, x] + cf_ref[1, x] + cf_ref[2, x] + below
        diagonal = diagonal + jnp.where(row == 0, cylo_v[x : x + 1], pltpu.roll(cf_ref[1, x], 1, 0))
        diagonal = diagonal + jnp.where(lane == 0, 0.0, pltpu.roll(cf_ref[2, x], 1, 1))
        res = rhs_ref[x] - applied[x]
        cell = res / diagonal
        d_ref[x] = cell
        rd = rd + res * cell
        g_ref[x] = 0.5 * guess[x]
    dplo[...] = d_ref[:, 0, :]
    dphi[...] = d_ref[:, BY - 1, :]
    d_sends = [
        send(d_ref.at[BX - 1], dxlo, 10, up_x),
        send(d_ref.at[0], dxup, 11, lo_x),
        send(dphi, dylo, 12, up_y),
        send(dplo, dyup, 13, lo_y),
    ]
    w_row = to_row(weights, 0)
    rest = proj - jnp.sum(gram * w_row, axis=1, keepdims=True)
    for copy in d_sends:
        copy.wait_recv()

    cells = [d_ref[x] for x in range(BX)]
    applied = apply(cells, dxlo[...], dxup[...], dylo[...], dyup[...])
    dad = zero
    for x in range(BX):
        dad = dad + cells[x] * applied[x]

    def fold(block):
        return jnp.sum(block[:, :HZ] + block[:, HZ:], axis=0, keepdims=True)

    for i in range(NV):
        acc = v_ref[i, 0] * applied[0]
        for x in range(1, BX):
            acc = acc + v_ref[i, x] * applied[x]
        proj_acc[i] = fold(acc)
    corr_col = jnp.sum(proj_acc[...].reshape(NV, HZ), axis=1, keepdims=True)
    line_at = lax.broadcasted_iota(jnp.int32, (1, 128), 1)
    value = to_row(corr_col, NV)
    value = jnp.where(line_at == 0, jnp.sum(fold(rd), axis=1, keepdims=True), value)
    value = jnp.where(line_at == 1, jnp.sum(fold(dad), axis=1, keepdims=True), value)
    value = stage(value, src2.at[0], a2c, 3, core, core_peers, 2)
    value = stage(value, src2.at[1], a2x, 4, xy, xy_peers, n_xy)
    value = stage(value, src2.at[2], a2z, 5, iy, z_peers, n_gy)

    shift = jnp.sum(inverse * value, axis=1, keepdims=True)
    wb[...] = jnp.broadcast_to(shift, (NV, 128))
    corr = to_col(value, NV)
    numerator = value[:, 0:1] - jnp.sum(shift * rest, axis=0, keepdims=True)
    denominator = value[:, 1:2] - jnp.sum(shift * corr, axis=0, keepdims=True)
    step = numerator / denominator
    update = [d_ref[x] for x in range(BX)]
    for i in range(NV):
        m = scale(i)
        for x in range(BX):
            update[x] = update[x] - m * v_ref[i, x]
    for x in range(BX):
        o_ref[x] = step * update[x]
    for copy in sent:
        copy.wait_send()
    for others, at in ar_waits:
        pltpu.make_async_copy(others, others, ar_send.at[at]).wait()


def solution(mesh):
    n_gx, n_gy = mesh.shape["gx"], mesh.shape["gy"]
    n_xy = n_gx // 2

    def on_device(basis, rhs, extra_diag, coeff):
        vm = pltpu.VMEM
        cell = (BX, BY, BZ)
        slab = (NV, 8, BZ)
        flat = (NV * BY, BX * BZ)
        face = (NV * BY, 2 * BZ)
        anywhere = pl.BlockSpec(memory_space=pl.ANY)
        half, change = pl.pallas_call(
            functools.partial(kernel, n_gx, n_gy),
            out_shape=[vm(cell, F32)] * 2,
            in_specs=[anywhere] * 4,
            out_specs=[pl.BlockSpec(memory_space=vm)] * 2,
            scratch_shapes=[
                vm((NV,) + cell, F32),
                vm(cell, F32),
                vm(cell, F32),
                vm((3,) + cell, F32),
            ]
            + [vm(flat, BF16)] * 4
            + [vm(face, BF16)] * 4
            + [vm(slab, F32)] * 6
            + [vm(cell, F32)] * 2
            + [vm((8, BZ), F32)] * 3
            + [
                vm((NV, 1, HZ), F32),
                vm((NV * BY, NV * BY), F32),
                vm((NV, 128), F32),
                vm(cell, F32),
            ]
            + [vm((8, BZ), F32)] * 6
            + [
                vm((3, ROWS, 128), F32),
                vm((3, 1, 128), F32),
                vm((2, ROWS, 128), F32),
                vm((n_xy, ROWS, 128), F32),
                vm((n_gy, ROWS, 128), F32),
                vm((2, 1, 128), F32),
                vm((n_xy, 1, 128), F32),
                vm((n_gy, 1, 128), F32),
                pltpu.SemaphoreType.DMA((CHUNKS + 3,)),
                pltpu.SemaphoreType.DMA((14,)),
                pltpu.SemaphoreType.DMA((14,)),
                pltpu.SemaphoreType.DMA((6,)),
                pltpu.SemaphoreType.DMA((6,)),
                pltpu.SemaphoreType.REGULAR((3,)),
            ],
            compiler_params=pltpu.CompilerParams(
                collective_id=0, has_side_effects=True, vmem_limit_bytes=63 << 20
            ),
        )(basis, rhs, extra_diag, coeff)
        return 2.0 * half, 2.0 * half + change

    placed = (
        P(None, "gx", "gy", None),
        P("gx", "gy", None),
        P("gx", "gy", None),
        P(None, "gx", "gy", None),
    )
    return jax.shard_map(
        on_device,
        mesh=mesh,
        in_specs=placed,
        out_specs=(P("gx", "gy", None), P("gx", "gy", None)),
        check_vma=False,
    )
```

```python
import functools

import jax
import jax.numpy as jnp
from jax import lax
from jax.experimental import pallas as pl
from jax.experimental.pallas import tpu as pltpu
from jax.sharding import PartitionSpec as P

MESH = pl.DeviceIdType.MESH
F32 = jnp.float32
BF16 = jnp.bfloat16
NV = 32
BX = 8
BY = 8
BZ = 256
HZ = 128
CHUNKS = 4
ROWS = 9
SIDE = 4
PIVOTS = 4


def split(value):
    high = value.astype(BF16)
    low = (value - high.astype(F32)).astype(BF16)
    return high, low


def dot_t(a, b):
    return lax.dot_general(a, b, (((1,), (1,)), ((), ())), preferred_element_type=F32)


def kernel(
    n_gx,
    n_gy,
    basis_hbm,
    rhs_hbm,
    extra_hbm,
    coeff_hbm,
    g_ref,
    o_ref,
    v_ref,
    rhs_ref,
    ext_ref,
    cf_ref,
    vh,
    vl,
    ah,
    al,
    fh,
    fl,
    gh,
    gl,
    pylo,
    pyhi,
    hxlo,
    hxup,
    hylo,
    hyup,
    cxm,
    cym,
    cpack,
    cxlo,
    cylo,
    proj_acc,
    prod,
    wb,
    d_ref,
    dplo,
    dphi,
    dxlo,
    dxup,
    dylo,
    dyup,
    src1,
    src2,
    a1c,
    a1x,
    a1z,
    a2c,
    a2x,
    a2z,
    load_sem,
    hs_send,
    hs_recv,
    ar_send,
    ar_recv,
    news,
):
    ix = lax.axis_index("gx")
    iy = lax.axis_index("gy")
    core = ix % 2
    xy = ix // 2
    n_xy = n_gx // 2
    side = SIDE
    up_x = ((ix + 1) % n_gx, iy)
    lo_x = ((ix + n_gx - 1) % n_gx, iy)
    up_y = (ix, (iy + 1) % n_gy)
    lo_y = (ix, (iy + n_gy - 1) % n_gy)
    x_at, y_at = xy % side, xy // side
    row_peers = [((y_at * side + (x_at + t) % side) * 2 + core, iy) for t in range(1, side)]
    column_peers = [
        (((y_at + t) % (n_xy // side) * side + x_at) * 2 + core, iy) for t in range(1, n_xy // side)
    ]
    z_at = {t: (ix, (iy + n_gy + t) % n_gy) for t in (-4, -2, -1, 1, 2, 4)}
    core_peers = [(xy * 2 + (core + 1) % 2, iy)]
    xy_peers = [(((xy + t) % n_xy) * 2 + core, iy) for t in range(1, n_xy)]
    z_peers = [(ix, (iy + t) % n_gy) for t in range(1, n_gy)]
    first_x, last_x = ix == 0, ix == n_gx - 1
    first_y, last_y = iy == 0, iy == n_gy - 1

    per = NV // CHUNKS
    loads = [
        pltpu.make_async_copy(coeff_hbm, cf_ref, load_sem.at[CHUNKS]),
        pltpu.make_async_copy(rhs_hbm, rhs_ref, load_sem.at[CHUNKS + 1]),
        pltpu.make_async_copy(extra_hbm, ext_ref, load_sem.at[CHUNKS + 2]),
    ]
    v_loads = [
        pltpu.make_async_copy(
            basis_hbm.at[pl.ds(k * per, per)], v_ref.at[pl.ds(k * per, per)], load_sem.at[k]
        )
        for k in range(CHUNKS)
    ]
    for copy in v_loads[:1] + loads + v_loads[1:]:
        copy.start()

    barrier = pltpu.get_barrier_semaphore()
    greeted = [up_x, lo_x] + [z_at[t] for t in (1, -1, 2, -2)]
    greeted = greeted + row_peers + column_peers + core_peers
    for peer in greeted:
        pl.semaphore_signal(barrier, inc=1, device_id=peer, device_id_type=MESH)

    row = lax.broadcasted_iota(jnp.int32, (BY, BZ), 0)
    lane = lax.broadcasted_iota(jnp.int32, (BY, BZ), 1)
    zero = jnp.zeros((BY, BZ), F32)

    def coefficient_masks():
        for x in range(BX):
            cxm[x] = cf_ref[0, x] if x < BX - 1 else jnp.where(last_x, cf_ref[0, x], 0.0)
            cym[x] = jnp.where(jnp.logical_or(row < BY - 1, last_y), cf_ref[1, x], 0.0)

    def local_pair(pair, carry):
        i0 = pair * 2
        base = pl.multiple_of(pair * 16, 16)
        flux_before = [None, None]
        acc = [jnp.zeros((BY, HZ), F32) for _ in range(2)]
        cells = [v_ref[i0 + s, 0] for s in range(2)]
        for x in range(BX):
            outs = []
            nexts = []
            for s in range(2):
                v = cells[s]
                v_up = v_ref[i0 + s, x + 1] if x < BX - 1 else zero
                nexts.append(v_up)
                flux = cxm[x] * (v - v_up)
                out = ext_ref[x] * v + flux
                if x > 0:
                    out = out - flux_before[s]
                flux_before[s] = flux
                v_up = jnp.where(row == BY - 1, 0.0, pltpu.roll(v, BY - 1, 0))
                flux = cym[x] * (v - v_up)
                out = out + flux - jnp.where(row == 0, 0.0, pltpu.roll(flux, 1, 0))
                v_up = jnp.where(lane == BZ - 1, 0.0, pltpu.roll(v, BZ - 1, 1))
                flux = cf_ref[2, x] * (v - v_up)
                out = out + flux - jnp.where(lane == 0, 0.0, pltpu.roll(flux, 1, 1))
                outs.append(out)
                term = v * rhs_ref[x]
                acc[s] = acc[s] + term[:, :HZ] + term[:, HZ:]
            rows, cols = pl.ds(base, 16), pl.ds(x * BZ, BZ)
            vh[rows, cols], vl[rows, cols] = split(jnp.concatenate(cells, axis=0))
            ah[rows, cols], al[rows, cols] = split(jnp.concatenate(outs, axis=0))
            cells = nexts
        for s in range(2):
            proj_acc[i0 + s] = jnp.sum(acc[s], axis=0, keepdims=True)
        return carry

    for k in range(CHUNKS):
        v_loads[k].wait()
        for i in range(k * per, (k + 1) * per):
            pylo[i] = v_ref[i, :, 0, :]
            pyhi[i] = v_ref[i, :, BY - 1, :]
    for copy in loads:
        copy.wait()
    cpack[...] = cf_ref[1, :, BY - 1, :]
    coefficient_masks()
    pl.semaphore_wait(barrier, len(greeted))

    def tell(peers, at):
        for peer in peers:
            pl.semaphore_signal(news.at[at], inc=1, device_id=peer, device_id_type=MESH)

    sent = []

    def send(src, dst, at, peer):
        copy = pltpu.make_async_remote_copy(
            src, dst, hs_send.at[at], hs_recv.at[at], device_id=peer, device_id_type=MESH
        )
        copy.start()
        sent.append(copy)
        return copy

    low, high = pl.ds(0, HZ), pl.ds(HZ, HZ)
    y_first = [
        send(pyhi.at[:, :, low], hylo.at[:, :, low], 2, up_y),
        send(pylo.at[:, :, high], hyup.at[:, :, high], 3, lo_y),
    ]
    x_first = [
        send(basis_hbm.at[:, BX - 1, :, low], hxlo.at[:, :, low], 0, up_x),
        send(basis_hbm.at[:, 0, :, high], hxup.at[:, :, high], 1, lo_x),
    ]

    c_sends = [
        send(cf_ref.at[0, BX - 1], cxlo, 4, up_x),
        send(cpack, cylo, 5, up_y),
    ]
    tell(row_peers, 0)
    tell([z_at[2], z_at[-2]], 1)

    lax.fori_loop(0, NV // 2, local_pair, 0)
    pl.semaphore_wait(news.at[0], len(row_peers))
    pl.semaphore_wait(news.at[1], 2)
    tell([z_at[4], z_at[-4]], 2)
    prod[...] = dot_t(vh[...], ah[...]) + dot_t(vh[...], al[...]) + dot_t(vl[...], ah[...])

    for copy in x_first + y_first + c_sends:
        copy.wait_recv()
    x_later = [
        send(basis_hbm.at[:, BX - 1, :, high], hxlo.at[:, :, high], 6, up_x),
        send(basis_hbm.at[:, 0, :, low], hxup.at[:, :, low], 7, lo_x),
    ]
    y_later = [
        send(pyhi.at[:, :, high], hylo.at[:, :, high], 8, up_y),
        send(pylo.at[:, :, low], hyup.at[:, :, low], 9, lo_y),
    ]
    cxlo_v = jnp.where(first_x, 0.0, cxlo[...])
    cylo_v = jnp.where(first_y, 0.0, cylo[...])
    cx_face = jnp.concatenate(
        [cxlo_v[:, :HZ], jnp.where(last_x, 0.0, cf_ref[0, BX - 1, :, HZ:])], axis=1
    )
    cy_face = jnp.concatenate([cylo_v[:, :HZ], jnp.where(last_y, 0.0, cpack[:, HZ:])], axis=1)
    for pair in range(NV // 2):
        for at, coef in ((0, cx_face), (1, cy_face)):
            diffs = []
            flows = []
            for i in (2 * pair, 2 * pair + 1):
                if at == 0:
                    a = v_ref[i, 0, :, :HZ] - hxlo[i, :, :HZ]
                    b = v_ref[i, BX - 1, :, HZ:] - hxup[i, :, HZ:]
                else:
                    a = pylo[i, :, :HZ] - hylo[i, :, :HZ]
                    b = pyhi[i, :, HZ:] - hyup[i, :, HZ:]
                diff = jnp.concatenate([a, b], axis=1)
                diffs.append(diff)
                flows.append(diff * coef)
            rows, cols = pl.ds(16 * pair, 16), pl.ds(at * BZ, BZ)
            fh[rows, cols], fl[rows, cols] = split(jnp.concatenate(diffs, axis=0))
            gh[rows, cols], gl[rows, cols] = split(jnp.concatenate(flows, axis=0))
    total = (
        prod[...] + dot_t(fh[...], gh[...]) + dot_t(fh[...], gl[...]) + dot_t(fl[...], gh[...])
    )
    same = (
        lax.broadcasted_iota(jnp.int32, (NV * BY, NV * BY), 0) % BY
        == lax.broadcasted_iota(jnp.int32, (NV * BY, NV * BY), 1) % BY
    )
    total = jnp.where(same, total, 0.0)
    sums = jnp.sum(total.reshape(NV, BY, NV * BY), axis=1)
    wide = jnp.concatenate([sums[8 * k : 8 * k + 8] for k in range(4)], axis=1)
    s_row = lax.broadcasted_iota(jnp.int32, (4 * NV * BY, 128), 0)
    s_col = lax.broadcasted_iota(jnp.int32, (4 * NV * BY, 128), 1)
    pick = (s_row // BY == s_col).astype(F32)
    packed = jnp.dot(wide, pick, precision=lax.Precision.HIGHEST, preferred_element_type=F32)

    eye_r = lax.broadcasted_iota(jnp.int32, (NV, 128), 0)
    eye_l = lax.broadcasted_iota(jnp.int32, (NV, 128), 1)

    def to_row(col, at):
        return jnp.sum(jnp.where(eye_l == eye_r + at, col, 0.0), axis=0, keepdims=True)

    def to_col(line, at):
        return jnp.sum(jnp.where(eye_l == eye_r + at, line, 0.0), axis=1, keepdims=True)

    proj_col = jnp.sum(proj_acc[...].reshape(NV, HZ), axis=1, keepdims=True)

    ar_waits = []

    def stage(value, src, buf, at, me, peers, count):
        src[...] = value
        for peer in peers:
            pltpu.make_async_remote_copy(
                src, buf.at[me], ar_send.at[at], ar_recv.at[at], device_id=peer, device_id_type=MESH
            ).start()
        buf[me] = value
        others = buf.at[pl.ds(0, count - 1)]
        pltpu.make_async_copy(others, others, ar_recv.at[at]).wait()
        ar_waits.append((others, at))
        return jnp.sum(buf[...], axis=0)

    value = jnp.concatenate([packed, to_row(proj_col, 0)], axis=0)
    value = stage(value, src1.at[0], a1c, 0, core, core_peers, 2)
    value = stage(value, src1.at[1], a1x, 1, xy, xy_peers, n_xy)
    pl.semaphore_wait(news.at[2], 2)
    value = stage(value, src1.at[2], a1z, 2, iy, z_peers, n_gy)

    gram = jnp.concatenate(
        [value[0:8]] + [pltpu.roll(value[0:8], 128 - 32 * k, 1) for k in range(1, 4)], axis=0
    )
    gram = jnp.where(eye_l < NV, gram, 0.0)
    proj = to_col(value[8:9], 0)
    mat = jnp.where(eye_l == eye_r + NV, 1.0, jnp.where(eye_l == 2 * NV, proj, gram))
    for k in range(0, NV, PIVOTS):
        cols = [jnp.broadcast_to(mat[:, k + j : k + j + 1], (NV, 128)) for j in range(PIVOTS)]
        rows = [mat[k + j : k + j + 1] for j in range(PIVOTS)]
        head = [[cols[j][k + i : k + i + 1] for j in range(PIVOTS)] for i in range(PIVOTS)]
        for j in range(PIVOTS):
            scaled = 1.0 / head[j][j]
            rows[j] = rows[j] * scaled
            for m in range(j + 1, PIVOTS):
                head[j][m] = head[j][m] * scaled
            for i in range(PIVOTS):
                if i != j:
                    rows[i] = rows[i] - head[i][j] * rows[j]
                    for m in range(j + 1, PIVOTS):
                        head[i][m] = head[i][m] - head[i][j] * head[j][m]
        for j in range(PIVOTS):
            mat = mat - cols[j] * rows[j]
        for j in range(PIVOTS):
            mat = jnp.where(eye_r == k + j, rows[j], mat)
    weights = mat[:, 2 * NV : 2 * NV + 1]
    inverse = jnp.where(jnp.logical_and(eye_l >= NV, eye_l < 2 * NV), mat, 0.0)
    wb[...] = jnp.broadcast_to(weights, (NV, 128))

    for copy in x_later + y_later:
        copy.wait_recv()

    def scale(i):
        line = wb[i : i + 1, :]
        return jnp.concatenate([line, line], axis=1)

    guess = [zero for _ in range(BX)]
    halo = [zero for _ in range(4)]
    for i in range(NV):
        w = scale(i)
        for x in range(BX):
            guess[x] = guess[x] + w * v_ref[i, x]
        for at, ref in enumerate((hxlo, hxup, hylo, hyup)):
            halo[at] = halo[at] + w * ref[i]

    def apply(cells, hx_lo, hx_up, hy_lo, hy_up):
        hx_up = jnp.where(last_x, 0.0, hx_up)
        hy_up = jnp.where(last_y, 0.0, hy_up)
        before = cxlo_v * (hx_lo - cells[0])
        outs = []
        for x in range(BX):
            v = cells[x]
            flux = cf_ref[0, x] * (v - (cells[x + 1] if x < BX - 1 else hx_up))
            out = ext_ref[x] * v + flux - before
            before = flux
            v_up = jnp.where(row == BY - 1, hy_up[x : x + 1], pltpu.roll(v, BY - 1, 0))
            flux = cf_ref[1, x] * (v - v_up)
            below = cylo_v[x : x + 1] * (hy_lo[x : x + 1] - v)
            out = out + flux - jnp.where(row == 0, below, pltpu.roll(flux, 1, 0))
            v_up = jnp.where(lane == BZ - 1, 0.0, pltpu.roll(v, BZ - 1, 1))
            flux = cf_ref[2, x] * (v - v_up)
            out = out + flux - jnp.where(lane == 0, 0.0, pltpu.roll(flux, 1, 1))
            outs.append(out)
        return outs

    applied = apply(guess, *halo)
    rd = zero
    for x in range(BX):
        below = cxlo_v if x == 0 else cf_ref[0, x - 1]
        diagonal = ext_ref[x] + cf_ref[0, x] + cf_ref[1, x] + cf_ref[2, x] + below
        diagonal = diagonal + jnp.where(row == 0, cylo_v[x : x + 1], pltpu.roll(cf_ref[1, x], 1, 0))
        diagonal = diagonal + jnp.where(lane == 0, 0.0, pltpu.roll(cf_ref[2, x], 1, 1))
        res = rhs_ref[x] - applied[x]
        cell = res / diagonal
        d_ref[x] = cell
        rd = rd + res * cell
        g_ref[x] = 0.5 * guess[x]
    dplo[...] = d_ref[:, 0, :]
    dphi[...] = d_ref[:, BY - 1, :]
    d_sends = [
        send(d_ref.at[BX - 1], dxlo, 10, up_x),
        send(d_ref.at[0], dxup, 11, lo_x),
        send(dphi, dylo, 12, up_y),
        send(dplo, dyup, 13, lo_y),
    ]
    w_row = to_row(weights, 0)
    rest = proj - jnp.sum(gram * w_row, axis=1, keepdims=True)
    for copy in d_sends:
        copy.wait_recv()

    cells = [d_ref[x] for x in range(BX)]
    applied = apply(cells, dxlo[...], dxup[...], dylo[...], dyup[...])
    dad = zero
    for x in range(BX):
        dad = dad + cells[x] * applied[x]

    def fold(block):
        return jnp.sum(block[:, :HZ] + block[:, HZ:], axis=0, keepdims=True)

    for i in range(NV):
        acc = v_ref[i, 0] * applied[0]
        for x in range(1, BX):
            acc = acc + v_ref[i, x] * applied[x]
        proj_acc[i] = fold(acc)
    corr_col = jnp.sum(proj_acc[...].reshape(NV, HZ), axis=1, keepdims=True)
    line_at = lax.broadcasted_iota(jnp.int32, (1, 128), 1)
    value = to_row(corr_col, NV)
    value = jnp.where(line_at == 0, jnp.sum(fold(rd), axis=1, keepdims=True), value)
    value = jnp.where(line_at == 1, jnp.sum(fold(dad), axis=1, keepdims=True), value)
    value = stage(value, src2.at[0], a2c, 3, core, core_peers, 2)
    value = stage(value, src2.at[1], a2x, 4, xy, xy_peers, n_xy)
    value = stage(value, src2.at[2], a2z, 5, iy, z_peers, n_gy)

    shift = jnp.sum(inverse * value, axis=1, keepdims=True)
    wb[...] = jnp.broadcast_to(shift, (NV, 128))
    corr = to_col(value, NV)
    numerator = value[:, 0:1] - jnp.sum(shift * rest, axis=0, keepdims=True)
    denominator = value[:, 1:2] - jnp.sum(shift * corr, axis=0, keepdims=True)
    step = numerator / denominator
    update = [d_ref[x] for x in range(BX)]
    for i in range(NV):
        m = scale(i)
        for x in range(BX):
            update[x] = update[x] - m * v_ref[i, x]
    for x in range(BX):
        o_ref[x] = step * update[x]
    for copy in sent:
        copy.wait_send()
    for others, at in ar_waits:
        pltpu.make_async_copy(others, others, ar_send.at[at]).wait()


def solution(mesh):
    n_gx, n_gy = mesh.shape["gx"], mesh.shape["gy"]
    n_xy = n_gx // 2

    def on_device(basis, rhs, extra_diag, coeff):
        vm = pltpu.VMEM
        cell = (BX, BY, BZ)
        slab = (NV, 8, BZ)
        flat = (NV * BY, BX * BZ)
        face = (NV * BY, 2 * BZ)
        anywhere = pl.BlockSpec(memory_space=pl.ANY)
        half, change = pl.pallas_call(
            functools.partial(kernel, n_gx, n_gy),
            out_shape=[vm(cell, F32)] * 2,
            in_specs=[anywhere] * 4,
            out_specs=[pl.BlockSpec(memory_space=vm)] * 2,
            scratch_shapes=[
                vm((NV,) + cell, F32),
                vm(cell, F32),
                vm(cell, F32),
                vm((3,) + cell, F32),
            ]
            + [vm(flat, BF16)] * 4
            + [vm(face, BF16)] * 4
            + [vm(slab, F32)] * 6
            + [vm(cell, F32)] * 2
            + [vm((8, BZ), F32)] * 3
            + [
                vm((NV, 1, HZ), F32),
                vm((NV * BY, NV * BY), F32),
                vm((NV, 128), F32),
                vm(cell, F32),
            ]
            + [vm((8, BZ), F32)] * 6
            + [
                vm((3, ROWS, 128), F32),
                vm((3, 1, 128), F32),
                vm((2, ROWS, 128), F32),
                vm((n_xy, ROWS, 128), F32),
                vm((n_gy, ROWS, 128), F32),
                vm((2, 1, 128), F32),
                vm((n_xy, 1, 128), F32),
                vm((n_gy, 1, 128), F32),
                pltpu.SemaphoreType.DMA((CHUNKS + 3,)),
                pltpu.SemaphoreType.DMA((14,)),
                pltpu.SemaphoreType.DMA((14,)),
                pltpu.SemaphoreType.DMA((6,)),
                pltpu.SemaphoreType.DMA((6,)),
                pltpu.SemaphoreType.REGULAR((3,)),
            ],
            compiler_params=pltpu.CompilerParams(
                collective_id=0, has_side_effects=True, vmem_limit_bytes=63 << 20
            ),
        )(basis, rhs, extra_diag, coeff)
        return 2.0 * half, 2.0 * half + change

    placed = (
        P(None, "gx", "gy", None),
        P("gx", "gy", None),
        P("gx", "gy", None),
        P(None, "gx", "gy", None),
    )
    return jax.shard_map(
        on_device,
        mesh=mesh,
        in_specs=placed,
        out_specs=(P("gx", "gy", None), P("gx", "gy", None)),
        check_vma=False,
    )
```

```python
import functools

import jax
import jax.numpy as jnp
from jax import lax
from jax.experimental import pallas as pl
from jax.experimental.pallas import tpu as pltpu
from jax.sharding import PartitionSpec as P

MESH = pl.DeviceIdType.MESH
F32 = jnp.float32
BF16 = jnp.bfloat16
NV = 32
BX = 8
BY = 8
BZ = 256
HZ = 128
CHUNKS = 4
ROWS = 9
SIDE = 4
PIVOTS = 4


def split(value):
    high = value.astype(BF16)
    low = (value - high.astype(F32)).astype(BF16)
    return high, low


def dot_t(a, b):
    return lax.dot_general(a, b, (((1,), (1,)), ((), ())), preferred_element_type=F32)


def kernel(
    n_gx,
    n_gy,
    basis_hbm,
    rhs_hbm,
    extra_hbm,
    coeff_hbm,
    g_ref,
    o_ref,
    v_ref,
    rhs_ref,
    ext_ref,
    cf_ref,
    vh,
    vl,
    ah,
    al,
    fh,
    fl,
    gh,
    gl,
    pylo,
    pyhi,
    hxlo,
    hxup,
    hylo,
    hyup,
    cxm,
    cym,
    cpack,
    cxlo,
    cylo,
    proj_acc,
    prod,
    wb,
    d_ref,
    dplo,
    dphi,
    bc,
    sx,
    sy,
    qx,
    qy,
    src1,
    src2,
    a1c,
    a1x,
    a1z,
    a2c,
    a2x,
    a2z,
    load_sem,
    hs_send,
    hs_recv,
    ar_send,
    ar_recv,
    news,
):
    ix = lax.axis_index("gx")
    iy = lax.axis_index("gy")
    core = ix % 2
    xy = ix // 2
    n_xy = n_gx // 2
    side = SIDE
    up_x = ((ix + 1) % n_gx, iy)
    lo_x = ((ix + n_gx - 1) % n_gx, iy)
    up_y = (ix, (iy + 1) % n_gy)
    lo_y = (ix, (iy + n_gy - 1) % n_gy)
    x_at, y_at = xy % side, xy // side
    row_peers = [((y_at * side + (x_at + t) % side) * 2 + core, iy) for t in range(1, side)]
    column_peers = [
        (((y_at + t) % (n_xy // side) * side + x_at) * 2 + core, iy) for t in range(1, n_xy // side)
    ]
    z_at = {t: (ix, (iy + n_gy + t) % n_gy) for t in (-4, -2, -1, 1, 2, 4)}
    core_peers = [(xy * 2 + (core + 1) % 2, iy)]
    xy_peers = [(((xy + t) % n_xy) * 2 + core, iy) for t in range(1, n_xy)]
    z_peers = [(ix, (iy + t) % n_gy) for t in range(1, n_gy)]
    first_x, last_x = ix == 0, ix == n_gx - 1
    first_y, last_y = iy == 0, iy == n_gy - 1

    per = NV // CHUNKS
    loads = [
        pltpu.make_async_copy(coeff_hbm, cf_ref, load_sem.at[CHUNKS]),
        pltpu.make_async_copy(rhs_hbm, rhs_ref, load_sem.at[CHUNKS + 1]),
        pltpu.make_async_copy(extra_hbm, ext_ref, load_sem.at[CHUNKS + 2]),
    ]
    v_loads = [
        pltpu.make_async_copy(
            basis_hbm.at[pl.ds(k * per, per)], v_ref.at[pl.ds(k * per, per)], load_sem.at[k]
        )
        for k in range(CHUNKS)
    ]
    for copy in v_loads[:1] + loads + v_loads[1:]:
        copy.start()

    barrier = pltpu.get_barrier_semaphore()
    greeted = [up_x, lo_x] + [z_at[t] for t in (1, -1, 2, -2)]
    greeted = greeted + row_peers + column_peers + core_peers
    for peer in greeted:
        pl.semaphore_signal(barrier, inc=1, device_id=peer, device_id_type=MESH)

    row = lax.broadcasted_iota(jnp.int32, (BY, BZ), 0)
    lane = lax.broadcasted_iota(jnp.int32, (BY, BZ), 1)
    zero = jnp.zeros((BY, BZ), F32)

    def coefficient_masks():
        for x in range(BX):
            cxm[x] = cf_ref[0, x] if x < BX - 1 else jnp.where(last_x, cf_ref[0, x], 0.0)
            cym[x] = jnp.where(jnp.logical_or(row < BY - 1, last_y), cf_ref[1, x], 0.0)

    def local_pair(pair, carry):
        i0 = pair * 2
        base = pl.multiple_of(pair * 16, 16)
        flux_before = [None, None]
        acc = [jnp.zeros((BY, HZ), F32) for _ in range(2)]
        cells = [v_ref[i0 + s, 0] for s in range(2)]
        for x in range(BX):
            outs = []
            nexts = []
            for s in range(2):
                v = cells[s]
                v_up = v_ref[i0 + s, x + 1] if x < BX - 1 else zero
                nexts.append(v_up)
                flux = cxm[x] * (v - v_up)
                out = ext_ref[x] * v + flux
                if x > 0:
                    out = out - flux_before[s]
                flux_before[s] = flux
                v_up = jnp.where(row == BY - 1, 0.0, pltpu.roll(v, BY - 1, 0))
                flux = cym[x] * (v - v_up)
                out = out + flux - jnp.where(row == 0, 0.0, pltpu.roll(flux, 1, 0))
                v_up = jnp.where(lane == BZ - 1, 0.0, pltpu.roll(v, BZ - 1, 1))
                flux = cf_ref[2, x] * (v - v_up)
                out = out + flux - jnp.where(lane == 0, 0.0, pltpu.roll(flux, 1, 1))
                outs.append(out)
                term = v * rhs_ref[x]
                acc[s] = acc[s] + term[:, :HZ] + term[:, HZ:]
            rows, cols = pl.ds(base, 16), pl.ds(x * BZ, BZ)
            vh[rows, cols], vl[rows, cols] = split(jnp.concatenate(cells, axis=0))
            ah[rows, cols], al[rows, cols] = split(jnp.concatenate(outs, axis=0))
            cells = nexts
        for s in range(2):
            proj_acc[i0 + s] = jnp.sum(acc[s], axis=0, keepdims=True)
        return carry

    for k in range(CHUNKS):
        v_loads[k].wait()
        for i in range(k * per, (k + 1) * per):
            pylo[i] = v_ref[i, :, 0, :]
            pyhi[i] = v_ref[i, :, BY - 1, :]
    for copy in loads:
        copy.wait()
    cpack[...] = cf_ref[1, :, BY - 1, :]
    coefficient_masks()
    pl.semaphore_wait(barrier, len(greeted))

    def tell(peers, at):
        for peer in peers:
            pl.semaphore_signal(news.at[at], inc=1, device_id=peer, device_id_type=MESH)

    sent = []

    def send(src, dst, at, peer):
        copy = pltpu.make_async_remote_copy(
            src, dst, hs_send.at[at], hs_recv.at[at], device_id=peer, device_id_type=MESH
        )
        copy.start()
        sent.append(copy)
        return copy

    low, high = pl.ds(0, HZ), pl.ds(HZ, HZ)
    y_first = [
        send(pyhi.at[:, :, low], hylo.at[:, :, low], 2, up_y),
        send(pylo.at[:, :, high], hyup.at[:, :, high], 3, lo_y),
    ]
    x_first = [
        send(basis_hbm.at[:, BX - 1, :, low], hxlo.at[:, :, low], 0, up_x),
        send(basis_hbm.at[:, 0, :, high], hxup.at[:, :, high], 1, lo_x),
    ]

    c_sends = [
        send(cf_ref.at[0, BX - 1], cxlo, 4, up_x),
        send(cpack, cylo, 5, up_y),
    ]
    tell(row_peers, 0)
    tell([z_at[2], z_at[-2]], 1)

    lax.fori_loop(0, NV // 2, local_pair, 0)
    pl.semaphore_wait(news.at[0], len(row_peers))
    pl.semaphore_wait(news.at[1], 2)
    tell([z_at[4], z_at[-4]], 2)
    prod[...] = dot_t(vh[...], ah[...]) + dot_t(vh[...], al[...]) + dot_t(vl[...], ah[...])

    for copy in x_first + y_first + c_sends:
        copy.wait_recv()
    x_later = [
        send(basis_hbm.at[:, BX - 1, :, high], hxlo.at[:, :, high], 6, up_x),
        send(basis_hbm.at[:, 0, :, low], hxup.at[:, :, low], 7, lo_x),
    ]
    y_later = [
        send(pyhi.at[:, :, high], hylo.at[:, :, high], 8, up_y),
        send(pylo.at[:, :, low], hyup.at[:, :, low], 9, lo_y),
    ]
    cxlo_v = jnp.where(first_x, 0.0, cxlo[...])
    cylo_v = jnp.where(first_y, 0.0, cylo[...])
    cx_face = jnp.concatenate(
        [cxlo_v[:, :HZ], jnp.where(last_x, 0.0, cf_ref[0, BX - 1, :, HZ:])], axis=1
    )
    cy_face = jnp.concatenate([cylo_v[:, :HZ], jnp.where(last_y, 0.0, cpack[:, HZ:])], axis=1)
    for pair in range(NV // 2):
        for at, coef in ((0, cx_face), (1, cy_face)):
            diffs = []
            flows = []
            for i in (2 * pair, 2 * pair + 1):
                if at == 0:
                    a = v_ref[i, 0, :, :HZ] - hxlo[i, :, :HZ]
                    b = v_ref[i, BX - 1, :, HZ:] - hxup[i, :, HZ:]
                else:
                    a = pylo[i, :, :HZ] - hylo[i, :, :HZ]
                    b = pyhi[i, :, HZ:] - hyup[i, :, HZ:]
                diff = jnp.concatenate([a, b], axis=1)
                diffs.append(diff)
                flows.append(diff * coef)
            rows, cols = pl.ds(16 * pair, 16), pl.ds(at * BZ, BZ)
            fh[rows, cols], fl[rows, cols] = split(jnp.concatenate(diffs, axis=0))
            gh[rows, cols], gl[rows, cols] = split(jnp.concatenate(flows, axis=0))
    total = (
        prod[...] + dot_t(fh[...], gh[...]) + dot_t(fh[...], gl[...]) + dot_t(fl[...], gh[...])
    )
    same = (
        lax.broadcasted_iota(jnp.int32, (NV * BY, NV * BY), 0) % BY
        == lax.broadcasted_iota(jnp.int32, (NV * BY, NV * BY), 1) % BY
    )
    total = jnp.where(same, total, 0.0)
    sums = jnp.sum(total.reshape(NV, BY, NV * BY), axis=1)
    wide = jnp.concatenate([sums[8 * k : 8 * k + 8] for k in range(4)], axis=1)
    s_row = lax.broadcasted_iota(jnp.int32, (4 * NV * BY, 128), 0)
    s_col = lax.broadcasted_iota(jnp.int32, (4 * NV * BY, 128), 1)
    pick = (s_row // BY == s_col).astype(F32)
    packed = jnp.dot(wide, pick, precision=lax.Precision.HIGHEST, preferred_element_type=F32)

    eye_r = lax.broadcasted_iota(jnp.int32, (NV, 128), 0)
    eye_l = lax.broadcasted_iota(jnp.int32, (NV, 128), 1)

    def to_row(col, at):
        return jnp.sum(jnp.where(eye_l == eye_r + at, col, 0.0), axis=0, keepdims=True)

    def to_col(line, at):
        return jnp.sum(jnp.where(eye_l == eye_r + at, line, 0.0), axis=1, keepdims=True)

    proj_col = jnp.sum(proj_acc[...].reshape(NV, HZ), axis=1, keepdims=True)

    def turned(v, low_edge, high_edge):
        return (
            jnp.where(row == 0, low_edge, pltpu.roll(v, 1, 0)),
            jnp.where(row == BY - 1, high_edge, pltpu.roll(v, BY - 1, 0)),
        )

    def along_z(v):
        return (
            jnp.where(lane == 0, 0.0, pltpu.roll(v, 1, 1)),
            jnp.where(lane == BZ - 1, 0.0, pltpu.roll(v, BZ - 1, 1)),
        )

    def edge(a):
        return 0 if a == 0 else BX - 1

    q_sends = []

    def boundary():
        for copy in x_later + y_later:
            copy.wait_recv()
        rights = []
        for side_at in range(2):
            a = edge(side_at)
            x_low = cxlo_v if a == 0 else cf_ref[0, a - 1]
            y_low = turned(cf_ref[1, a], cylo_v[a : a + 1], 0.0)[0]
            z_low = along_z(cf_ref[2, a])[0]
            faces = [x_low, cf_ref[0, a], y_low, cf_ref[1, a], z_low, cf_ref[2, a]]
            faces.append(ext_ref[a])
            inverse_d = 1.0 / sum(faces[1:], faces[0])
            for m, face in enumerate(faces):
                bc[side_at, m] = face
            bc[side_at, 7] = inverse_d
            rights.append(rhs_ref[a] * inverse_d)
        for side_at in range(2):
            b = edge(side_at)
            c_x = cf_ref[0, :, b, :]
            x_low = turned(c_x, cxlo_v[b : b + 1], 0.0)[0]
            y_low = cylo_v if b == 0 else cf_ref[1, :, b - 1, :]
            c_z = cf_ref[2, :, b, :]
            faces = [x_low, c_x, y_low, cf_ref[1, :, b, :], along_z(c_z)[0], c_z]
            faces.append(ext_ref[:, b, :])
            inverse_d = 1.0 / sum(faces[1:], faces[0])
            for m, face in enumerate(faces):
                bc[2 + side_at, m] = face
            bc[2 + side_at, 7] = inverse_d
            rights.append(rhs_ref[:, b, :] * inverse_d)

        def meet(at, v, near):
            out = bc[at, 6] * v
            for m, other in enumerate(near):
                out = out + bc[at, m] * (v - other)
            return out * bc[at, 7]

        def one(i, carry):
            x_lo, y_lo = hxlo[i], hylo[i]
            x_up = jnp.where(last_x, 0.0, hxup[i])
            y_up = jnp.where(last_y, 0.0, hyup[i])
            found = []
            for at in range(2):
                a = edge(at)
                v = v_ref[i, a]
                x_near = (x_lo, v_ref[i, 1]) if a == 0 else (v_ref[i, a - 1], x_up)
                y_near = turned(v, y_lo[a : a + 1], y_up[a : a + 1])
                found.append(meet(at, v, x_near + y_near + along_z(v)))
            for at in range(2):
                b = edge(at)
                v = pylo[i] if b == 0 else pyhi[i]
                y_near = (y_lo, v_ref[i, :, 1, :]) if b == 0 else (v_ref[i, :, b - 1, :], y_up)
                x_near = turned(v, x_lo[b : b + 1], x_up[b : b + 1])
                found.append(meet(2 + at, v, x_near + y_near + along_z(v)))
            sx[i] = jnp.concatenate([found[1][:, :HZ], found[0][:, HZ:]], axis=1)
            sy[i] = jnp.concatenate([found[3][:, :HZ], found[2][:, HZ:]], axis=1)
            return carry

        lax.fori_loop(0, NV, one, 0)
        sx[NV] = jnp.concatenate([rights[1][:, :HZ], rights[0][:, HZ:]], axis=1)
        sy[NV] = jnp.concatenate([rights[3][:, :HZ], rights[2][:, HZ:]], axis=1)
        q_sends.extend(
            [
                send(sy.at[:, :, low], qy.at[:, :, low], 12, up_y),
                send(sy.at[:, :, high], qy.at[:, :, high], 13, lo_y),
                send(sx.at[:, :, low], qx.at[:, :, low], 10, up_x),
                send(sx.at[:, :, high], qx.at[:, :, high], 11, lo_x),
            ]
        )

    ar_waits = []

    def stage(value, src, buf, at, me, peers, count, meanwhile=None):
        src[...] = value
        for peer in peers:
            pltpu.make_async_remote_copy(
                src, buf.at[me], ar_send.at[at], ar_recv.at[at], device_id=peer, device_id_type=MESH
            ).start()
        buf[me] = value
        if meanwhile is not None:
            meanwhile()
        others = buf.at[pl.ds(0, count - 1)]
        pltpu.make_async_copy(others, others, ar_recv.at[at]).wait()
        ar_waits.append((others, at))
        return jnp.sum(buf[...], axis=0)

    value = jnp.concatenate([packed, to_row(proj_col, 0)], axis=0)
    value = stage(value, src1.at[0], a1c, 0, core, core_peers, 2)
    value = stage(value, src1.at[1], a1x, 1, xy, xy_peers, n_xy)
    pl.semaphore_wait(news.at[2], 2)
    value = stage(value, src1.at[2], a1z, 2, iy, z_peers, n_gy, boundary)

    gram = jnp.concatenate(
        [value[0:8]] + [pltpu.roll(value[0:8], 128 - 32 * k, 1) for k in range(1, 4)], axis=0
    )
    gram = jnp.where(eye_l < NV, gram, 0.0)
    proj = to_col(value[8:9], 0)
    mat = jnp.where(eye_l == eye_r + NV, 1.0, jnp.where(eye_l == 2 * NV, proj, gram))
    for k in range(0, NV, PIVOTS):
        cols = [jnp.broadcast_to(mat[:, k + j : k + j + 1], (NV, 128)) for j in range(PIVOTS)]
        rows = [mat[k + j : k + j + 1] for j in range(PIVOTS)]
        head = [[cols[j][k + i : k + i + 1] for j in range(PIVOTS)] for i in range(PIVOTS)]
        for j in range(PIVOTS):
            scaled = 1.0 / head[j][j]
            rows[j] = rows[j] * scaled
            for m in range(j + 1, PIVOTS):
                head[j][m] = head[j][m] * scaled
            for i in range(PIVOTS):
                if i != j:
                    rows[i] = rows[i] - head[i][j] * rows[j]
                    for m in range(j + 1, PIVOTS):
                        head[i][m] = head[i][m] - head[i][j] * head[j][m]
        for j in range(PIVOTS):
            mat = mat - cols[j] * rows[j]
        for j in range(PIVOTS):
            mat = jnp.where(eye_r == k + j, rows[j], mat)
    weights = mat[:, 2 * NV : 2 * NV + 1]
    inverse = jnp.where(jnp.logical_and(eye_l >= NV, eye_l < 2 * NV), mat, 0.0)
    wb[...] = jnp.broadcast_to(weights, (NV, 128))

    for copy in q_sends:
        copy.wait_recv()

    def scale(i):
        line = wb[i : i + 1, :]
        return jnp.concatenate([line, line], axis=1)

    guess = [zero for _ in range(BX)]
    halo = [zero for _ in range(4)]
    beyond = [qx[NV], qy[NV]]
    for i in range(NV):
        w = scale(i)
        for x in range(BX):
            guess[x] = guess[x] + w * v_ref[i, x]
        for at, ref in enumerate((hxlo, hxup, hylo, hyup)):
            halo[at] = halo[at] + w * ref[i]
        beyond = [beyond[0] - w * qx[i], beyond[1] - w * qy[i]]

    def apply(cells, hx_lo, hx_up, hy_lo, hy_up):
        hx_up = jnp.where(last_x, 0.0, hx_up)
        hy_up = jnp.where(last_y, 0.0, hy_up)
        before = cxlo_v * (hx_lo - cells[0])
        outs = []
        for x in range(BX):
            v = cells[x]
            flux = cf_ref[0, x] * (v - (cells[x + 1] if x < BX - 1 else hx_up))
            out = ext_ref[x] * v + flux - before
            before = flux
            v_up = jnp.where(row == BY - 1, hy_up[x : x + 1], pltpu.roll(v, BY - 1, 0))
            flux = cf_ref[1, x] * (v - v_up)
            below = cylo_v[x : x + 1] * (hy_lo[x : x + 1] - v)
            out = out + flux - jnp.where(row == 0, below, pltpu.roll(flux, 1, 0))
            v_up = jnp.where(lane == BZ - 1, 0.0, pltpu.roll(v, BZ - 1, 1))
            flux = cf_ref[2, x] * (v - v_up)
            out = out + flux - jnp.where(lane == 0, 0.0, pltpu.roll(flux, 1, 1))
            outs.append(out)
        return outs

    def apply_inside(cells):
        before = zero
        outs = []
        for x in range(BX):
            v = cells[x]
            flux = cxm[x] * (v - (cells[x + 1] if x < BX - 1 else zero))
            out = ext_ref[x] * v + flux - before
            before = flux
            flux = cym[x] * (v - turned(v, 0.0, 0.0)[1])
            out = out + flux - turned(flux, 0.0, 0.0)[0]
            flux = cf_ref[2, x] * (v - along_z(v)[1])
            out = out + flux - along_z(flux)[0]
            outs.append(out)
        return outs

    applied = apply(guess, *halo)
    rd = zero
    for x in range(BX):
        below = cxlo_v if x == 0 else cf_ref[0, x - 1]
        diagonal = ext_ref[x] + cf_ref[0, x] + cf_ref[1, x] + cf_ref[2, x] + below
        diagonal = diagonal + jnp.where(row == 0, cylo_v[x : x + 1], pltpu.roll(cf_ref[1, x], 1, 0))
        diagonal = diagonal + jnp.where(lane == 0, 0.0, pltpu.roll(cf_ref[2, x], 1, 1))
        res = rhs_ref[x] - applied[x]
        cell = res / diagonal
        d_ref[x] = cell
        rd = rd + res * cell
        g_ref[x] = 0.5 * guess[x]
    dplo[...] = d_ref[:, 0, :]
    dphi[...] = d_ref[:, BY - 1, :]
    w_row = to_row(weights, 0)
    rest = proj - jnp.sum(gram * w_row, axis=1, keepdims=True)

    cells = [d_ref[x] for x in range(BX)]
    applied = apply_inside(cells)
    jump_x = jnp.concatenate([cells[0][:, :HZ], cells[BX - 1][:, HZ:]], axis=1) - beyond[0]
    jump_y = jnp.concatenate([dplo[:, :HZ], dphi[:, HZ:]], axis=1) - beyond[1]
    flow_x, flow_y = cx_face * jump_x, cy_face * jump_y
    dad = flow_x * jump_x + flow_y * jump_y
    for x in range(BX):
        dad = dad + cells[x] * applied[x]

    def fold(block):
        return jnp.sum(block[:, :HZ] + block[:, HZ:], axis=0, keepdims=True)

    for i in range(NV):
        acc = v_ref[i, 0] * applied[0]
        for x in range(1, BX):
            acc = acc + v_ref[i, x] * applied[x]
        diff_x = [v_ref[i, 0, :, :HZ] - hxlo[i, :, :HZ], v_ref[i, BX - 1, :, HZ:] - hxup[i, :, HZ:]]
        diff_y = [pylo[i, :, :HZ] - hylo[i, :, :HZ], pyhi[i, :, HZ:] - hyup[i, :, HZ:]]
        acc = acc + flow_x * jnp.concatenate(diff_x, axis=1)
        acc = acc + flow_y * jnp.concatenate(diff_y, axis=1)
        proj_acc[i] = fold(acc)
    corr_col = jnp.sum(proj_acc[...].reshape(NV, HZ), axis=1, keepdims=True)
    line_at = lax.broadcasted_iota(jnp.int32, (1, 128), 1)
    value = to_row(corr_col, NV)
    value = jnp.where(line_at == 0, jnp.sum(fold(rd), axis=1, keepdims=True), value)
    value = jnp.where(line_at == 1, jnp.sum(fold(dad), axis=1, keepdims=True), value)
    value = stage(value, src2.at[0], a2c, 3, core, core_peers, 2)
    value = stage(value, src2.at[1], a2x, 4, xy, xy_peers, n_xy)
    value = stage(value, src2.at[2], a2z, 5, iy, z_peers, n_gy)

    shift = jnp.sum(inverse * value, axis=1, keepdims=True)
    wb[...] = jnp.broadcast_to(shift, (NV, 128))
    corr = to_col(value, NV)
    numerator = value[:, 0:1] - jnp.sum(shift * rest, axis=0, keepdims=True)
    denominator = value[:, 1:2] - jnp.sum(shift * corr, axis=0, keepdims=True)
    step = numerator / denominator
    update = [d_ref[x] for x in range(BX)]
    for i in range(NV):
        m = scale(i)
        for x in range(BX):
            update[x] = update[x] - m * v_ref[i, x]
    for x in range(BX):
        o_ref[x] = step * update[x]
    for copy in sent:
        copy.wait_send()
    for others, at in ar_waits:
        pltpu.make_async_copy(others, others, ar_send.at[at]).wait()


def solution(mesh):
    n_gx, n_gy = mesh.shape["gx"], mesh.shape["gy"]
    n_xy = n_gx // 2

    def on_device(basis, rhs, extra_diag, coeff):
        vm = pltpu.VMEM
        cell = (BX, BY, BZ)
        slab = (NV, 8, BZ)
        flat = (NV * BY, BX * BZ)
        face = (NV * BY, 2 * BZ)
        anywhere = pl.BlockSpec(memory_space=pl.ANY)
        half, change = pl.pallas_call(
            functools.partial(kernel, n_gx, n_gy),
            out_shape=[vm(cell, F32)] * 2,
            in_specs=[anywhere] * 4,
            out_specs=[pl.BlockSpec(memory_space=vm)] * 2,
            scratch_shapes=[
                vm((NV,) + cell, F32),
                vm(cell, F32),
                vm(cell, F32),
                vm((3,) + cell, F32),
            ]
            + [vm(flat, BF16)] * 4
            + [vm(face, BF16)] * 4
            + [vm(slab, F32)] * 6
            + [vm(cell, F32)] * 2
            + [vm((8, BZ), F32)] * 3
            + [
                vm((NV, 1, HZ), F32),
                vm((NV * BY, NV * BY), F32),
                vm((NV, 128), F32),
                vm(cell, F32),
            ]
            + [vm((8, BZ), F32)] * 2
            + [vm((4, 8, 8, BZ), F32)]
            + [vm((NV + 1, 8, BZ), F32)] * 4
            + [
                vm((3, ROWS, 128), F32),
                vm((3, 1, 128), F32),
                vm((2, ROWS, 128), F32),
                vm((n_xy, ROWS, 128), F32),
                vm((n_gy, ROWS, 128), F32),
                vm((2, 1, 128), F32),
                vm((n_xy, 1, 128), F32),
                vm((n_gy, 1, 128), F32),
                pltpu.SemaphoreType.DMA((CHUNKS + 3,)),
                pltpu.SemaphoreType.DMA((14,)),
                pltpu.SemaphoreType.DMA((14,)),
                pltpu.SemaphoreType.DMA((6,)),
                pltpu.SemaphoreType.DMA((6,)),
                pltpu.SemaphoreType.REGULAR((3,)),
            ],
            compiler_params=pltpu.CompilerParams(
                collective_id=0, has_side_effects=True, vmem_limit_bytes=63 << 20
            ),
        )(basis, rhs, extra_diag, coeff)
        return 2.0 * half, 2.0 * half + change

    placed = (
        P(None, "gx", "gy", None),
        P("gx", "gy", None),
        P("gx", "gy", None),
        P(None, "gx", "gy", None),
    )
    return jax.shard_map(
        on_device,
        mesh=mesh,
        in_specs=placed,
        out_specs=(P("gx", "gy", None), P("gx", "gy", None)),
        check_vma=False,
    )
```

```python
import functools

import jax
import jax.numpy as jnp
from jax import lax
from jax.experimental import pallas as pl
from jax.experimental.pallas import tpu as pltpu
from jax.sharding import PartitionSpec as P

MESH = pl.DeviceIdType.MESH
F32 = jnp.float32
BF16 = jnp.bfloat16
NV = 32
BX = 8
BY = 8
BZ = 256
HZ = 128
CHUNKS = 4
ROWS = 9
SIDE = 4
PIVOTS = 4


def split(value):
    high = value.astype(BF16)
    low = (value - high.astype(F32)).astype(BF16)
    return high, low


def dot_t(a, b):
    return lax.dot_general(a, b, (((1,), (1,)), ((), ())), preferred_element_type=F32)


def kernel(
    n_gx,
    n_gy,
    basis_hbm,
    rhs_hbm,
    extra_hbm,
    coeff_hbm,
    g_ref,
    o_ref,
    v_ref,
    rhs_ref,
    ext_ref,
    cf_ref,
    vh,
    vl,
    ah,
    al,
    fh,
    fl,
    gh,
    gl,
    pylo,
    pyhi,
    hxlo,
    hxup,
    hylo,
    hyup,
    cxm,
    cym,
    cpack,
    cxlo,
    cylo,
    proj_acc,
    prod,
    wb,
    d_ref,
    dplo,
    dphi,
    bc,
    sx,
    sy,
    qx,
    qy,
    src1,
    src2,
    a1x,
    a1z,
    a2x,
    a2z,
    load_sem,
    hs_send,
    hs_recv,
    ar_send,
    ar_recv,
    news,
):
    ix = lax.axis_index("gx")
    iy = lax.axis_index("gy")
    core = ix % 2
    xy = ix // 2
    n_xy = n_gx // 2
    side = SIDE
    up_x = ((ix + 1) % n_gx, iy)
    lo_x = ((ix + n_gx - 1) % n_gx, iy)
    up_y = (ix, (iy + 1) % n_gy)
    lo_y = (ix, (iy + n_gy - 1) % n_gy)
    x_at, y_at = xy % side, xy // side
    row_peers = [((y_at * side + (x_at + t) % side) * 2 + core, iy) for t in range(1, side)]
    column_peers = [
        (((y_at + t) % (n_xy // side) * side + x_at) * 2 + core, iy) for t in range(1, n_xy // side)
    ]
    z_at = {t: (ix, (iy + n_gy + t) % n_gy) for t in (-4, -2, -1, 1, 2, 4)}
    core_peers = [(xy * 2 + (core + 1) % 2, iy)]
    tall = n_xy // side

    def steps(count):
        return sorted(range(count), key=lambda t: -min(t, count - t))

    hops = [(b, a, c) for b in range(tall) for a in range(side) for c in range(2) if a + b + c]
    hops.sort(key=lambda t: -(min(t[0], tall - t[0]) + min(t[1], side - t[1])))
    plane_peers = [
        ((((y_at + b) % tall) * side + (x_at + a) % side) * 2 + (core + c) % 2, iy)
        for b, a, c in hops
    ]
    z_peers = [(ix, (iy + t) % n_gy) for t in steps(n_gy) if t]
    first_x, last_x = ix == 0, ix == n_gx - 1
    first_y, last_y = iy == 0, iy == n_gy - 1

    per = NV // CHUNKS
    loads = [
        pltpu.make_async_copy(coeff_hbm, cf_ref, load_sem.at[CHUNKS]),
        pltpu.make_async_copy(rhs_hbm, rhs_ref, load_sem.at[CHUNKS + 1]),
        pltpu.make_async_copy(extra_hbm, ext_ref, load_sem.at[CHUNKS + 2]),
    ]
    v_loads = [
        pltpu.make_async_copy(
            basis_hbm.at[pl.ds(k * per, per)], v_ref.at[pl.ds(k * per, per)], load_sem.at[k]
        )
        for k in range(CHUNKS)
    ]
    for copy in v_loads[:1] + loads + v_loads[1:]:
        copy.start()

    barrier = pltpu.get_barrier_semaphore()
    greeted = [up_x, lo_x] + [z_at[t] for t in (1, -1, 2, -2)]
    greeted = greeted + row_peers + column_peers + core_peers
    for peer in greeted:
        pl.semaphore_signal(barrier, inc=1, device_id=peer, device_id_type=MESH)

    row = lax.broadcasted_iota(jnp.int32, (BY, BZ), 0)
    lane = lax.broadcasted_iota(jnp.int32, (BY, BZ), 1)
    zero = jnp.zeros((BY, BZ), F32)

    def coefficient_masks():
        for x in range(BX):
            cxm[x] = cf_ref[0, x] if x < BX - 1 else jnp.where(last_x, cf_ref[0, x], 0.0)
            cym[x] = jnp.where(jnp.logical_or(row < BY - 1, last_y), cf_ref[1, x], 0.0)

    def local_pair(pair, carry):
        i0 = pair * 2
        base = pl.multiple_of(pair * 16, 16)
        flux_before = [None, None]
        acc = [jnp.zeros((BY, HZ), F32) for _ in range(2)]
        cells = [v_ref[i0 + s, 0] for s in range(2)]
        for x in range(BX):
            outs = []
            nexts = []
            for s in range(2):
                v = cells[s]
                v_up = v_ref[i0 + s, x + 1] if x < BX - 1 else zero
                nexts.append(v_up)
                flux = cxm[x] * (v - v_up)
                out = ext_ref[x] * v + flux
                if x > 0:
                    out = out - flux_before[s]
                flux_before[s] = flux
                v_up = jnp.where(row == BY - 1, 0.0, pltpu.roll(v, BY - 1, 0))
                flux = cym[x] * (v - v_up)
                out = out + flux - jnp.where(row == 0, 0.0, pltpu.roll(flux, 1, 0))
                v_up = jnp.where(lane == BZ - 1, 0.0, pltpu.roll(v, BZ - 1, 1))
                flux = cf_ref[2, x] * (v - v_up)
                out = out + flux - jnp.where(lane == 0, 0.0, pltpu.roll(flux, 1, 1))
                outs.append(out)
                term = v * rhs_ref[x]
                acc[s] = acc[s] + term[:, :HZ] + term[:, HZ:]
            rows, cols = pl.ds(base, 16), pl.ds(x * BZ, BZ)
            vh[rows, cols], vl[rows, cols] = split(jnp.concatenate(cells, axis=0))
            ah[rows, cols], al[rows, cols] = split(jnp.concatenate(outs, axis=0))
            cells = nexts
        for s in range(2):
            proj_acc[i0 + s] = jnp.sum(acc[s], axis=0, keepdims=True)
        return carry

    for k in range(CHUNKS):
        v_loads[k].wait()
        for i in range(k * per, (k + 1) * per):
            pylo[i] = v_ref[i, :, 0, :]
            pyhi[i] = v_ref[i, :, BY - 1, :]
    for copy in loads:
        copy.wait()
    cpack[...] = cf_ref[1, :, BY - 1, :]
    coefficient_masks()
    pl.semaphore_wait(barrier, len(greeted))

    def tell(peers, at):
        for peer in peers:
            pl.semaphore_signal(news.at[at], inc=1, device_id=peer, device_id_type=MESH)

    sent = []

    def send(src, dst, at, peer):
        copy = pltpu.make_async_remote_copy(
            src, dst, hs_send.at[at], hs_recv.at[at], device_id=peer, device_id_type=MESH
        )
        copy.start()
        sent.append(copy)
        return copy

    low, high = pl.ds(0, HZ), pl.ds(HZ, HZ)
    y_first = [
        send(pyhi.at[:, :, low], hylo.at[:, :, low], 2, up_y),
        send(pylo.at[:, :, high], hyup.at[:, :, high], 3, lo_y),
    ]
    x_first = [
        send(basis_hbm.at[:, BX - 1, :, low], hxlo.at[:, :, low], 0, up_x),
        send(basis_hbm.at[:, 0, :, high], hxup.at[:, :, high], 1, lo_x),
    ]

    c_sends = [
        send(cf_ref.at[0, BX - 1], cxlo, 4, up_x),
        send(cpack, cylo, 5, up_y),
    ]
    tell(row_peers, 0)
    tell([z_at[2], z_at[-2]], 1)

    lax.fori_loop(0, NV // 2, local_pair, 0)
    pl.semaphore_wait(news.at[0], len(row_peers))
    pl.semaphore_wait(news.at[1], 2)
    tell([z_at[4], z_at[-4]], 2)
    tell(core_peers, 3)
    prod[...] = dot_t(vh[...], ah[...]) + dot_t(vh[...], al[...]) + dot_t(vl[...], ah[...])

    for copy in x_first + y_first + c_sends:
        copy.wait_recv()
    x_later = [
        send(basis_hbm.at[:, BX - 1, :, high], hxlo.at[:, :, high], 6, up_x),
        send(basis_hbm.at[:, 0, :, low], hxup.at[:, :, low], 7, lo_x),
    ]
    y_later = [
        send(pyhi.at[:, :, high], hylo.at[:, :, high], 8, up_y),
        send(pylo.at[:, :, low], hyup.at[:, :, low], 9, lo_y),
    ]
    cxlo_v = jnp.where(first_x, 0.0, cxlo[...])
    cylo_v = jnp.where(first_y, 0.0, cylo[...])
    cx_face = jnp.concatenate(
        [cxlo_v[:, :HZ], jnp.where(last_x, 0.0, cf_ref[0, BX - 1, :, HZ:])], axis=1
    )
    cy_face = jnp.concatenate([cylo_v[:, :HZ], jnp.where(last_y, 0.0, cpack[:, HZ:])], axis=1)
    for pair in range(NV // 2):
        for at, coef in ((0, cx_face), (1, cy_face)):
            diffs = []
            flows = []
            for i in (2 * pair, 2 * pair + 1):
                if at == 0:
                    a = v_ref[i, 0, :, :HZ] - hxlo[i, :, :HZ]
                    b = v_ref[i, BX - 1, :, HZ:] - hxup[i, :, HZ:]
                else:
                    a = pylo[i, :, :HZ] - hylo[i, :, :HZ]
                    b = pyhi[i, :, HZ:] - hyup[i, :, HZ:]
                diff = jnp.concatenate([a, b], axis=1)
                diffs.append(diff)
                flows.append(diff * coef)
            rows, cols = pl.ds(16 * pair, 16), pl.ds(at * BZ, BZ)
            fh[rows, cols], fl[rows, cols] = split(jnp.concatenate(diffs, axis=0))
            gh[rows, cols], gl[rows, cols] = split(jnp.concatenate(flows, axis=0))
    total = (
        prod[...] + dot_t(fh[...], gh[...]) + dot_t(fh[...], gl[...]) + dot_t(fl[...], gh[...])
    )
    same = (
        lax.broadcasted_iota(jnp.int32, (NV * BY, NV * BY), 0) % BY
        == lax.broadcasted_iota(jnp.int32, (NV * BY, NV * BY), 1) % BY
    )
    total = jnp.where(same, total, 0.0)
    sums = jnp.sum(total.reshape(NV, BY, NV * BY), axis=1)
    wide = jnp.concatenate([sums[8 * k : 8 * k + 8] for k in range(4)], axis=1)
    s_row = lax.broadcasted_iota(jnp.int32, (4 * NV * BY, 128), 0)
    s_col = lax.broadcasted_iota(jnp.int32, (4 * NV * BY, 128), 1)
    pick = (s_row // BY == s_col).astype(F32)
    packed = jnp.dot(wide, pick, precision=lax.Precision.HIGHEST, preferred_element_type=F32)

    eye_r = lax.broadcasted_iota(jnp.int32, (NV, 128), 0)
    eye_l = lax.broadcasted_iota(jnp.int32, (NV, 128), 1)

    def to_row(col, at):
        return jnp.sum(jnp.where(eye_l == eye_r + at, col, 0.0), axis=0, keepdims=True)

    def to_col(line, at):
        return jnp.sum(jnp.where(eye_l == eye_r + at, line, 0.0), axis=1, keepdims=True)

    proj_col = jnp.sum(proj_acc[...].reshape(NV, HZ), axis=1, keepdims=True)

    def turned(v, low_edge, high_edge):
        return (
            jnp.where(row == 0, low_edge, pltpu.roll(v, 1, 0)),
            jnp.where(row == BY - 1, high_edge, pltpu.roll(v, BY - 1, 0)),
        )

    def along_z(v):
        return (
            jnp.where(lane == 0, 0.0, pltpu.roll(v, 1, 1)),
            jnp.where(lane == BZ - 1, 0.0, pltpu.roll(v, BZ - 1, 1)),
        )

    def edge(a):
        return 0 if a == 0 else BX - 1

    q_sends = []

    def boundary():
        for copy in x_later + y_later:
            copy.wait_recv()
        rights = []
        for side_at in range(2):
            a = edge(side_at)
            x_low = cxlo_v if a == 0 else cf_ref[0, a - 1]
            y_low = turned(cf_ref[1, a], cylo_v[a : a + 1], 0.0)[0]
            z_low = along_z(cf_ref[2, a])[0]
            faces = [x_low, cf_ref[0, a], y_low, cf_ref[1, a], z_low, cf_ref[2, a]]
            faces.append(ext_ref[a])
            inverse_d = 1.0 / sum(faces[1:], faces[0])
            for m, face in enumerate(faces):
                bc[side_at, m] = face
            bc[side_at, 7] = inverse_d
            rights.append(rhs_ref[a] * inverse_d)
        for side_at in range(2):
            b = edge(side_at)
            c_x = cf_ref[0, :, b, :]
            x_low = turned(c_x, cxlo_v[b : b + 1], 0.0)[0]
            y_low = cylo_v if b == 0 else cf_ref[1, :, b - 1, :]
            c_z = cf_ref[2, :, b, :]
            faces = [x_low, c_x, y_low, cf_ref[1, :, b, :], along_z(c_z)[0], c_z]
            faces.append(ext_ref[:, b, :])
            inverse_d = 1.0 / sum(faces[1:], faces[0])
            for m, face in enumerate(faces):
                bc[2 + side_at, m] = face
            bc[2 + side_at, 7] = inverse_d
            rights.append(rhs_ref[:, b, :] * inverse_d)

        def meet(at, v, near):
            out = bc[at, 6] * v
            for m, other in enumerate(near):
                out = out + bc[at, m] * (v - other)
            return out * bc[at, 7]

        def one(i, carry):
            x_lo, y_lo = hxlo[i], hylo[i]
            x_up = jnp.where(last_x, 0.0, hxup[i])
            y_up = jnp.where(last_y, 0.0, hyup[i])
            found = []
            for at in range(2):
                a = edge(at)
                v = v_ref[i, a]
                x_near = (x_lo, v_ref[i, 1]) if a == 0 else (v_ref[i, a - 1], x_up)
                y_near = turned(v, y_lo[a : a + 1], y_up[a : a + 1])
                found.append(meet(at, v, x_near + y_near + along_z(v)))
            for at in range(2):
                b = edge(at)
                v = pylo[i] if b == 0 else pyhi[i]
                y_near = (y_lo, v_ref[i, :, 1, :]) if b == 0 else (v_ref[i, :, b - 1, :], y_up)
                x_near = turned(v, x_lo[b : b + 1], x_up[b : b + 1])
                found.append(meet(2 + at, v, x_near + y_near + along_z(v)))
            sx[i] = jnp.concatenate([found[1][:, :HZ], found[0][:, HZ:]], axis=1)
            sy[i] = jnp.concatenate([found[3][:, :HZ], found[2][:, HZ:]], axis=1)
            return carry

        lax.fori_loop(0, NV, one, 0)
        sx[NV] = jnp.concatenate([rights[1][:, :HZ], rights[0][:, HZ:]], axis=1)
        sy[NV] = jnp.concatenate([rights[3][:, :HZ], rights[2][:, HZ:]], axis=1)
        q_sends.extend(
            [
                send(sy.at[:, :, low], qy.at[:, :, low], 12, up_y),
                send(sy.at[:, :, high], qy.at[:, :, high], 13, lo_y),
                send(sx.at[:, :, low], qx.at[:, :, low], 10, up_x),
                send(sx.at[:, :, high], qx.at[:, :, high], 11, lo_x),
            ]
        )

    ar_waits = []

    def stage(value, src, buf, at, me, peers, count, meanwhile=None):
        src[...] = value
        for peer in peers:
            pltpu.make_async_remote_copy(
                src, buf.at[me], ar_send.at[at], ar_recv.at[at], device_id=peer, device_id_type=MESH
            ).start()
        buf[me] = value
        if meanwhile is not None:
            meanwhile()
        others = buf.at[pl.ds(0, count - 1)]
        pltpu.make_async_copy(others, others, ar_recv.at[at]).wait()
        ar_waits.append((others, at))
        return jnp.sum(buf[...], axis=0)

    value = jnp.concatenate([packed, to_row(proj_col, 0)], axis=0)
    pl.semaphore_wait(news.at[3], 1)
    value = stage(value, src1.at[1], a1x, 1, ix, plane_peers, n_gx)
    pl.semaphore_wait(news.at[2], 2)
    value = stage(value, src1.at[2], a1z, 2, iy, z_peers, n_gy, boundary)

    gram = jnp.concatenate(
        [value[0:8]] + [pltpu.roll(value[0:8], 128 - 32 * k, 1) for k in range(1, 4)], axis=0
    )
    gram = jnp.where(eye_l < NV, gram, 0.0)
    proj = to_col(value[8:9], 0)
    mat = jnp.where(eye_l == eye_r + NV, 1.0, jnp.where(eye_l == 2 * NV, proj, gram))
    for k in range(0, NV, PIVOTS):
        cols = [jnp.broadcast_to(mat[:, k + j : k + j + 1], (NV, 128)) for j in range(PIVOTS)]
        rows = [mat[k + j : k + j + 1] for j in range(PIVOTS)]
        head = [[cols[j][k + i : k + i + 1] for j in range(PIVOTS)] for i in range(PIVOTS)]
        for j in range(PIVOTS):
            scaled = 1.0 / head[j][j]
            rows[j] = rows[j] * scaled
            for m in range(j + 1, PIVOTS):
                head[j][m] = head[j][m] * scaled
            for i in range(PIVOTS):
                if i != j:
                    rows[i] = rows[i] - head[i][j] * rows[j]
                    for m in range(j + 1, PIVOTS):
                        head[i][m] = head[i][m] - head[i][j] * head[j][m]
        for j in range(PIVOTS):
            mat = mat - cols[j] * rows[j]
        for j in range(PIVOTS):
            mat = jnp.where(eye_r == k + j, rows[j], mat)
    weights = mat[:, 2 * NV : 2 * NV + 1]
    inverse = jnp.where(jnp.logical_and(eye_l >= NV, eye_l < 2 * NV), mat, 0.0)
    wb[...] = jnp.broadcast_to(weights, (NV, 128))

    for copy in q_sends:
        copy.wait_recv()

    def scale(i):
        line = wb[i : i + 1, :]
        return jnp.concatenate([line, line], axis=1)

    guess = [zero for _ in range(BX)]
    halo = [zero for _ in range(4)]
    beyond = [qx[NV], qy[NV]]
    for i in range(NV):
        w = scale(i)
        for x in range(BX):
            guess[x] = guess[x] + w * v_ref[i, x]
        for at, ref in enumerate((hxlo, hxup, hylo, hyup)):
            halo[at] = halo[at] + w * ref[i]
        beyond = [beyond[0] - w * qx[i], beyond[1] - w * qy[i]]

    def apply(cells, hx_lo, hx_up, hy_lo, hy_up):
        hx_up = jnp.where(last_x, 0.0, hx_up)
        hy_up = jnp.where(last_y, 0.0, hy_up)
        before = cxlo_v * (hx_lo - cells[0])
        outs = []
        for x in range(BX):
            v = cells[x]
            flux = cf_ref[0, x] * (v - (cells[x + 1] if x < BX - 1 else hx_up))
            out = ext_ref[x] * v + flux - before
            before = flux
            v_up = jnp.where(row == BY - 1, hy_up[x : x + 1], pltpu.roll(v, BY - 1, 0))
            flux = cf_ref[1, x] * (v - v_up)
            below = cylo_v[x : x + 1] * (hy_lo[x : x + 1] - v)
            out = out + flux - jnp.where(row == 0, below, pltpu.roll(flux, 1, 0))
            v_up = jnp.where(lane == BZ - 1, 0.0, pltpu.roll(v, BZ - 1, 1))
            flux = cf_ref[2, x] * (v - v_up)
            out = out + flux - jnp.where(lane == 0, 0.0, pltpu.roll(flux, 1, 1))
            outs.append(out)
        return outs

    def apply_inside(cells):
        before = zero
        outs = []
        for x in range(BX):
            v = cells[x]
            flux = cxm[x] * (v - (cells[x + 1] if x < BX - 1 else zero))
            out = ext_ref[x] * v + flux - before
            before = flux
            flux = cym[x] * (v - turned(v, 0.0, 0.0)[1])
            out = out + flux - turned(flux, 0.0, 0.0)[0]
            flux = cf_ref[2, x] * (v - along_z(v)[1])
            out = out + flux - along_z(flux)[0]
            outs.append(out)
        return outs

    applied = apply(guess, *halo)
    rd = zero
    for x in range(BX):
        below = cxlo_v if x == 0 else cf_ref[0, x - 1]
        diagonal = ext_ref[x] + cf_ref[0, x] + cf_ref[1, x] + cf_ref[2, x] + below
        diagonal = diagonal + jnp.where(row == 0, cylo_v[x : x + 1], pltpu.roll(cf_ref[1, x], 1, 0))
        diagonal = diagonal + jnp.where(lane == 0, 0.0, pltpu.roll(cf_ref[2, x], 1, 1))
        res = rhs_ref[x] - applied[x]
        cell = res / diagonal
        d_ref[x] = cell
        rd = rd + res * cell
        g_ref[x] = 0.5 * guess[x]
    dplo[...] = d_ref[:, 0, :]
    dphi[...] = d_ref[:, BY - 1, :]
    w_row = to_row(weights, 0)
    rest = proj - jnp.sum(gram * w_row, axis=1, keepdims=True)

    cells = [d_ref[x] for x in range(BX)]
    applied = apply_inside(cells)
    jump_x = jnp.concatenate([cells[0][:, :HZ], cells[BX - 1][:, HZ:]], axis=1) - beyond[0]
    jump_y = jnp.concatenate([dplo[:, :HZ], dphi[:, HZ:]], axis=1) - beyond[1]
    flow_x, flow_y = cx_face * jump_x, cy_face * jump_y
    dad = flow_x * jump_x + flow_y * jump_y
    for x in range(BX):
        dad = dad + cells[x] * applied[x]

    def fold(block):
        return jnp.sum(block[:, :HZ] + block[:, HZ:], axis=0, keepdims=True)

    for i in range(NV):
        acc = v_ref[i, 0] * applied[0]
        for x in range(1, BX):
            acc = acc + v_ref[i, x] * applied[x]
        diff_x = [v_ref[i, 0, :, :HZ] - hxlo[i, :, :HZ], v_ref[i, BX - 1, :, HZ:] - hxup[i, :, HZ:]]
        diff_y = [pylo[i, :, :HZ] - hylo[i, :, :HZ], pyhi[i, :, HZ:] - hyup[i, :, HZ:]]
        acc = acc + flow_x * jnp.concatenate(diff_x, axis=1)
        acc = acc + flow_y * jnp.concatenate(diff_y, axis=1)
        proj_acc[i] = fold(acc)
    corr_col = jnp.sum(proj_acc[...].reshape(NV, HZ), axis=1, keepdims=True)
    line_at = lax.broadcasted_iota(jnp.int32, (1, 128), 1)
    value = to_row(corr_col, NV)
    value = jnp.where(line_at == 0, jnp.sum(fold(rd), axis=1, keepdims=True), value)
    value = jnp.where(line_at == 1, jnp.sum(fold(dad), axis=1, keepdims=True), value)
    value = stage(value, src2.at[1], a2x, 4, ix, plane_peers, n_gx)
    value = stage(value, src2.at[2], a2z, 5, iy, z_peers, n_gy)

    shift = jnp.sum(inverse * value, axis=1, keepdims=True)
    wb[...] = jnp.broadcast_to(shift, (NV, 128))
    corr = to_col(value, NV)
    numerator = value[:, 0:1] - jnp.sum(shift * rest, axis=0, keepdims=True)
    denominator = value[:, 1:2] - jnp.sum(shift * corr, axis=0, keepdims=True)
    step = numerator / denominator
    update = [d_ref[x] for x in range(BX)]
    for i in range(NV):
        m = scale(i)
        for x in range(BX):
            update[x] = update[x] - m * v_ref[i, x]
    for x in range(BX):
        o_ref[x] = step * update[x]
    for copy in sent:
        copy.wait_send()
    for others, at in ar_waits:
        pltpu.make_async_copy(others, others, ar_send.at[at]).wait()


def solution(mesh):
    n_gx, n_gy = mesh.shape["gx"], mesh.shape["gy"]
    n_xy = n_gx // 2

    def on_device(basis, rhs, extra_diag, coeff):
        vm = pltpu.VMEM
        cell = (BX, BY, BZ)
        slab = (NV, 8, BZ)
        flat = (NV * BY, BX * BZ)
        face = (NV * BY, 2 * BZ)
        anywhere = pl.BlockSpec(memory_space=pl.ANY)
        half, change = pl.pallas_call(
            functools.partial(kernel, n_gx, n_gy),
            out_shape=[vm(cell, F32)] * 2,
            in_specs=[anywhere] * 4,
            out_specs=[pl.BlockSpec(memory_space=vm)] * 2,
            scratch_shapes=[
                vm((NV,) + cell, F32),
                vm(cell, F32),
                vm(cell, F32),
                vm((3,) + cell, F32),
            ]
            + [vm(flat, BF16)] * 4
            + [vm(face, BF16)] * 4
            + [vm(slab, F32)] * 6
            + [vm(cell, F32)] * 2
            + [vm((8, BZ), F32)] * 3
            + [
                vm((NV, 1, HZ), F32),
                vm((NV * BY, NV * BY), F32),
                vm((NV, 128), F32),
                vm(cell, F32),
            ]
            + [vm((8, BZ), F32)] * 2
            + [vm((4, 8, 8, BZ), F32)]
            + [vm((NV + 1, 8, BZ), F32)] * 4
            + [
                vm((3, ROWS, 128), F32),
                vm((3, 1, 128), F32),
                vm((n_gx, ROWS, 128), F32),
                vm((n_gy, ROWS, 128), F32),
                vm((n_gx, 1, 128), F32),
                vm((n_gy, 1, 128), F32),
                pltpu.SemaphoreType.DMA((CHUNKS + 3,)),
                pltpu.SemaphoreType.DMA((14,)),
                pltpu.SemaphoreType.DMA((14,)),
                pltpu.SemaphoreType.DMA((6,)),
                pltpu.SemaphoreType.DMA((6,)),
                pltpu.SemaphoreType.REGULAR((4,)),
            ],
            compiler_params=pltpu.CompilerParams(
                collective_id=0, has_side_effects=True, vmem_limit_bytes=63 << 20
            ),
        )(basis, rhs, extra_diag, coeff)
        return 2.0 * half, 2.0 * half + change

    placed = (
        P(None, "gx", "gy", None),
        P("gx", "gy", None),
        P("gx", "gy", None),
        P(None, "gx", "gy", None),
    )
    return jax.shard_map(
        on_device,
        mesh=mesh,
        in_specs=placed,
        out_specs=(P("gx", "gy", None), P("gx", "gy", None)),
        check_vma=False,
    )
```

```python
import functools

import jax
import jax.numpy as jnp
from jax import lax
from jax.experimental import pallas as pl
from jax.experimental.pallas import tpu as pltpu
from jax.sharding import PartitionSpec as P

MESH = pl.DeviceIdType.MESH
F32 = jnp.float32
BF16 = jnp.bfloat16
NV = 32
BX = 8
BY = 8
BZ = 256
HZ = 128
CHUNKS = 4
ROWS = 9
SIDE = 4
PIVOTS = 4


def split(value):
    high = value.astype(BF16)
    low = (value - high.astype(F32)).astype(BF16)
    return high, low


def dot_t(a, b):
    return lax.dot_general(a, b, (((1,), (1,)), ((), ())), preferred_element_type=F32)


def kernel(
    n_gx,
    n_gy,
    basis_hbm,
    rhs_hbm,
    extra_hbm,
    coeff_hbm,
    g_ref,
    o_ref,
    v_ref,
    rhs_ref,
    ext_ref,
    cf_ref,
    vh,
    vl,
    ah,
    al,
    fh,
    fl,
    gh,
    gl,
    pylo,
    pyhi,
    hxlo,
    hxup,
    hylo,
    hyup,
    cxm,
    cym,
    cpack,
    cxlo,
    cylo,
    proj_acc,
    prod,
    wb,
    d_ref,
    dplo,
    dphi,
    bc,
    sx,
    sy,
    qx,
    qy,
    src1,
    src2,
    a1x,
    a1z,
    a2x,
    a2z,
    load_sem,
    hs_send,
    hs_recv,
    ar_send,
    ar_recv,
    news,
    pick,
):
    ix = lax.axis_index("gx")
    iy = lax.axis_index("gy")
    core = ix % 2
    xy = ix // 2
    n_xy = n_gx // 2
    side = SIDE
    up_x = ((ix + 1) % n_gx, iy)
    lo_x = ((ix + n_gx - 1) % n_gx, iy)
    up_y = (ix, (iy + 1) % n_gy)
    lo_y = (ix, (iy + n_gy - 1) % n_gy)
    x_at, y_at = xy % side, xy // side
    row_peers = [((y_at * side + (x_at + t) % side) * 2 + core, iy) for t in range(1, side)]
    column_peers = [
        (((y_at + t) % (n_xy // side) * side + x_at) * 2 + core, iy) for t in range(1, n_xy // side)
    ]
    z_at = {t: (ix, (iy + n_gy + t) % n_gy) for t in (-4, -2, -1, 1, 2, 4)}
    core_peers = [(xy * 2 + (core + 1) % 2, iy)]
    tall = n_xy // side

    def steps(count):
        return sorted(range(count), key=lambda t: -min(t, count - t))

    hops = [(b, a, c) for b in range(tall) for a in range(side) for c in range(2) if a + b + c]
    hops.sort(key=lambda t: -(min(t[0], tall - t[0]) + min(t[1], side - t[1])))
    plane_peers = [
        ((((y_at + b) % tall) * side + (x_at + a) % side) * 2 + (core + c) % 2, iy)
        for b, a, c in hops
    ]
    z_peers = [(ix, (iy + t) % n_gy) for t in steps(n_gy) if t]
    first_x, last_x = ix == 0, ix == n_gx - 1
    first_y, last_y = iy == 0, iy == n_gy - 1

    per = NV // CHUNKS
    loads = [
        pltpu.make_async_copy(coeff_hbm, cf_ref, load_sem.at[CHUNKS]),
        pltpu.make_async_copy(rhs_hbm, rhs_ref, load_sem.at[CHUNKS + 1]),
        pltpu.make_async_copy(extra_hbm, ext_ref, load_sem.at[CHUNKS + 2]),
    ]
    v_loads = [
        pltpu.make_async_copy(
            basis_hbm.at[pl.ds(k * per, per)], v_ref.at[pl.ds(k * per, per)], load_sem.at[k]
        )
        for k in range(CHUNKS)
    ]
    for copy in v_loads[:1] + loads + v_loads[1:]:
        copy.start()

    barrier = pltpu.get_barrier_semaphore()
    greeted = [up_x, lo_x] + [z_at[t] for t in (1, -1, 2, -2)]
    greeted = greeted + row_peers + column_peers + core_peers
    for peer in greeted:
        pl.semaphore_signal(barrier, inc=1, device_id=peer, device_id_type=MESH)

    row = lax.broadcasted_iota(jnp.int32, (BY, BZ), 0)
    lane = lax.broadcasted_iota(jnp.int32, (BY, BZ), 1)
    zero = jnp.zeros((BY, BZ), F32)

    def coefficient_masks():
        for x in range(BX):
            cxm[x] = cf_ref[0, x] if x < BX - 1 else jnp.where(last_x, cf_ref[0, x], 0.0)
            cym[x] = jnp.where(jnp.logical_or(row < BY - 1, last_y), cf_ref[1, x], 0.0)

    def local_pair(pair, carry):
        i0 = pair * 2
        base = pl.multiple_of(pair * 16, 16)
        flux_before = [None, None]
        acc = [jnp.zeros((BY, HZ), F32) for _ in range(2)]
        cells = [v_ref[i0 + s, 0] for s in range(2)]
        for x in range(BX):
            outs = []
            nexts = []
            for s in range(2):
                v = cells[s]
                v_up = v_ref[i0 + s, x + 1] if x < BX - 1 else zero
                nexts.append(v_up)
                flux = cxm[x] * (v - v_up)
                out = ext_ref[x] * v + flux
                if x > 0:
                    out = out - flux_before[s]
                flux_before[s] = flux
                v_up = jnp.where(row == BY - 1, 0.0, pltpu.roll(v, BY - 1, 0))
                flux = cym[x] * (v - v_up)
                out = out + flux - jnp.where(row == 0, 0.0, pltpu.roll(flux, 1, 0))
                v_up = jnp.where(lane == BZ - 1, 0.0, pltpu.roll(v, BZ - 1, 1))
                flux = cf_ref[2, x] * (v - v_up)
                out = out + flux - jnp.where(lane == 0, 0.0, pltpu.roll(flux, 1, 1))
                outs.append(out)
                term = v * rhs_ref[x]
                acc[s] = acc[s] + term[:, :HZ] + term[:, HZ:]
            rows, cols = pl.ds(base, 16), pl.ds(x * BZ, BZ)
            vh[rows, cols], vl[rows, cols] = split(jnp.concatenate(cells, axis=0))
            ah[rows, cols], al[rows, cols] = split(jnp.concatenate(outs, axis=0))
            cells = nexts
        for s in range(2):
            proj_acc[i0 + s] = jnp.sum(acc[s], axis=0, keepdims=True)
        return carry

    for k in range(CHUNKS):
        v_loads[k].wait()
        for i in range(k * per, (k + 1) * per):
            pylo[i] = v_ref[i, :, 0, :]
            pyhi[i] = v_ref[i, :, BY - 1, :]
    for copy in loads:
        copy.wait()
    cpack[...] = cf_ref[1, :, BY - 1, :]
    coefficient_masks()
    pl.semaphore_wait(barrier, len(greeted))

    def tell(peers, at):
        for peer in peers:
            pl.semaphore_signal(news.at[at], inc=1, device_id=peer, device_id_type=MESH)

    sent = []

    def send(src, dst, at, peer):
        copy = pltpu.make_async_remote_copy(
            src, dst, hs_send.at[at], hs_recv.at[at], device_id=peer, device_id_type=MESH
        )
        copy.start()
        sent.append(copy)
        return copy

    low, high = pl.ds(0, HZ), pl.ds(HZ, HZ)
    y_first = [
        send(pyhi.at[:, :, low], hylo.at[:, :, low], 2, up_y),
        send(pylo.at[:, :, high], hyup.at[:, :, high], 3, lo_y),
    ]
    x_first = [
        send(basis_hbm.at[:, BX - 1, :, low], hxlo.at[:, :, low], 0, up_x),
        send(basis_hbm.at[:, 0, :, high], hxup.at[:, :, high], 1, lo_x),
    ]

    c_sends = [
        send(cf_ref.at[0, BX - 1], cxlo, 4, up_x),
        send(cpack, cylo, 5, up_y),
    ]
    tell(row_peers, 0)
    tell([z_at[2], z_at[-2]], 1)

    lax.fori_loop(0, NV // 2, local_pair, 0)
    pl.semaphore_wait(news.at[0], len(row_peers))
    pl.semaphore_wait(news.at[1], 2)
    tell([z_at[4], z_at[-4]], 2)
    tell(core_peers, 3)
    prod[...] = dot_t(vh[...], ah[...]) + dot_t(vh[...], al[...]) + dot_t(vl[...], ah[...])

    s_row = lax.broadcasted_iota(jnp.int32, (4 * NV * BY, 128), 0)
    s_col = lax.broadcasted_iota(jnp.int32, (4 * NV * BY, 128), 1)
    pick[...] = (s_row // BY == s_col).astype(F32).astype(BF16)
    eye_r = lax.broadcasted_iota(jnp.int32, (NV, 128), 0)
    eye_l = lax.broadcasted_iota(jnp.int32, (NV, 128), 1)

    def to_row(col, at):
        return jnp.sum(jnp.where(eye_l == eye_r + at, col, 0.0), axis=0, keepdims=True)

    def to_col(line, at):
        return jnp.sum(jnp.where(eye_l == eye_r + at, line, 0.0), axis=1, keepdims=True)

    proj_col = jnp.sum(proj_acc[...].reshape(NV, HZ), axis=1, keepdims=True)
    proj_row = to_row(proj_col, 0)

    for copy in x_first + y_first + c_sends:
        copy.wait_recv()
    x_later = [
        send(basis_hbm.at[:, BX - 1, :, high], hxlo.at[:, :, high], 6, up_x),
        send(basis_hbm.at[:, 0, :, low], hxup.at[:, :, low], 7, lo_x),
    ]
    y_later = [
        send(pyhi.at[:, :, high], hylo.at[:, :, high], 8, up_y),
        send(pylo.at[:, :, low], hyup.at[:, :, low], 9, lo_y),
    ]
    cxlo_v = jnp.where(first_x, 0.0, cxlo[...])
    cylo_v = jnp.where(first_y, 0.0, cylo[...])
    cx_face = jnp.concatenate(
        [cxlo_v[:, :HZ], jnp.where(last_x, 0.0, cf_ref[0, BX - 1, :, HZ:])], axis=1
    )
    cy_face = jnp.concatenate([cylo_v[:, :HZ], jnp.where(last_y, 0.0, cpack[:, HZ:])], axis=1)
    for pair in range(NV // 2):
        for at, coef in ((0, cx_face), (1, cy_face)):
            diffs = []
            flows = []
            for i in (2 * pair, 2 * pair + 1):
                if at == 0:
                    a = v_ref[i, 0, :, :HZ] - hxlo[i, :, :HZ]
                    b = v_ref[i, BX - 1, :, HZ:] - hxup[i, :, HZ:]
                else:
                    a = pylo[i, :, :HZ] - hylo[i, :, :HZ]
                    b = pyhi[i, :, HZ:] - hyup[i, :, HZ:]
                diff = jnp.concatenate([a, b], axis=1)
                diffs.append(diff)
                flows.append(diff * coef)
            rows, cols = pl.ds(16 * pair, 16), pl.ds(at * BZ, BZ)
            fh[rows, cols], fl[rows, cols] = split(jnp.concatenate(diffs, axis=0))
            gh[rows, cols], gl[rows, cols] = split(jnp.concatenate(flows, axis=0))
    total = (
        prod[...] + dot_t(fh[...], gh[...]) + dot_t(fh[...], gl[...]) + dot_t(fl[...], gh[...])
    )
    same = (
        lax.broadcasted_iota(jnp.int32, (NV * BY, NV * BY), 0) % BY
        == lax.broadcasted_iota(jnp.int32, (NV * BY, NV * BY), 1) % BY
    )
    total = jnp.where(same, total, 0.0)
    sums = jnp.sum(total.reshape(NV, BY, NV * BY), axis=1)
    wide = jnp.concatenate([sums[8 * k : 8 * k + 8] for k in range(4)], axis=1)
    first, second = split(wide)
    third = (wide - first.astype(F32) - second.astype(F32)).astype(BF16)
    packed = sum(
        jnp.dot(part, pick[...], preferred_element_type=F32) for part in (third, second, first)
    )


    def turned(v, low_edge, high_edge):
        return (
            jnp.where(row == 0, low_edge, pltpu.roll(v, 1, 0)),
            jnp.where(row == BY - 1, high_edge, pltpu.roll(v, BY - 1, 0)),
        )

    def along_z(v):
        return (
            jnp.where(lane == 0, 0.0, pltpu.roll(v, 1, 1)),
            jnp.where(lane == BZ - 1, 0.0, pltpu.roll(v, BZ - 1, 1)),
        )

    def edge(a):
        return 0 if a == 0 else BX - 1

    q_sends = []

    def boundary():
        for copy in x_later + y_later:
            copy.wait_recv()
        rights = []
        for side_at in range(2):
            a = edge(side_at)
            x_low = cxlo_v if a == 0 else cf_ref[0, a - 1]
            y_low = turned(cf_ref[1, a], cylo_v[a : a + 1], 0.0)[0]
            z_low = along_z(cf_ref[2, a])[0]
            faces = [x_low, cf_ref[0, a], y_low, cf_ref[1, a], z_low, cf_ref[2, a]]
            faces.append(ext_ref[a])
            inverse_d = 1.0 / sum(faces[1:], faces[0])
            for m, face in enumerate(faces):
                bc[side_at, m] = face
            bc[side_at, 7] = inverse_d
            rights.append(rhs_ref[a] * inverse_d)
        for side_at in range(2):
            b = edge(side_at)
            c_x = cf_ref[0, :, b, :]
            x_low = turned(c_x, cxlo_v[b : b + 1], 0.0)[0]
            y_low = cylo_v if b == 0 else cf_ref[1, :, b - 1, :]
            c_z = cf_ref[2, :, b, :]
            faces = [x_low, c_x, y_low, cf_ref[1, :, b, :], along_z(c_z)[0], c_z]
            faces.append(ext_ref[:, b, :])
            inverse_d = 1.0 / sum(faces[1:], faces[0])
            for m, face in enumerate(faces):
                bc[2 + side_at, m] = face
            bc[2 + side_at, 7] = inverse_d
            rights.append(rhs_ref[:, b, :] * inverse_d)

        def meet(at, v, near):
            out = bc[at, 6] * v
            for m, other in enumerate(near):
                out = out + bc[at, m] * (v - other)
            return out * bc[at, 7]

        def one(i, carry):
            x_lo, y_lo = hxlo[i], hylo[i]
            x_up = jnp.where(last_x, 0.0, hxup[i])
            y_up = jnp.where(last_y, 0.0, hyup[i])
            found = []
            for at in range(2):
                a = edge(at)
                v = v_ref[i, a]
                x_near = (x_lo, v_ref[i, 1]) if a == 0 else (v_ref[i, a - 1], x_up)
                y_near = turned(v, y_lo[a : a + 1], y_up[a : a + 1])
                found.append(meet(at, v, x_near + y_near + along_z(v)))
            for at in range(2):
                b = edge(at)
                v = pylo[i] if b == 0 else pyhi[i]
                y_near = (y_lo, v_ref[i, :, 1, :]) if b == 0 else (v_ref[i, :, b - 1, :], y_up)
                x_near = turned(v, x_lo[b : b + 1], x_up[b : b + 1])
                found.append(meet(2 + at, v, x_near + y_near + along_z(v)))
            sx[i] = jnp.concatenate([found[1][:, :HZ], found[0][:, HZ:]], axis=1)
            sy[i] = jnp.concatenate([found[3][:, :HZ], found[2][:, HZ:]], axis=1)
            return carry

        lax.fori_loop(0, NV, one, 0)
        sx[NV] = jnp.concatenate([rights[1][:, :HZ], rights[0][:, HZ:]], axis=1)
        sy[NV] = jnp.concatenate([rights[3][:, :HZ], rights[2][:, HZ:]], axis=1)
        q_sends.extend(
            [
                send(sy.at[:, :, low], qy.at[:, :, low], 12, up_y),
                send(sy.at[:, :, high], qy.at[:, :, high], 13, lo_y),
                send(sx.at[:, :, low], qx.at[:, :, low], 10, up_x),
                send(sx.at[:, :, high], qx.at[:, :, high], 11, lo_x),
            ]
        )

    ar_waits = []

    def stage(value, src, buf, at, me, peers, count, meanwhile=None):
        src[...] = value
        for peer in peers:
            pltpu.make_async_remote_copy(
                src, buf.at[me], ar_send.at[at], ar_recv.at[at], device_id=peer, device_id_type=MESH
            ).start()
        buf[me] = value
        if meanwhile is not None:
            meanwhile()
        others = buf.at[pl.ds(0, count - 1)]
        pltpu.make_async_copy(others, others, ar_recv.at[at]).wait()
        ar_waits.append((others, at))
        return jnp.sum(buf[...], axis=0)

    value = jnp.concatenate([packed, proj_row], axis=0)
    pl.semaphore_wait(news.at[3], 1)
    value = stage(value, src1.at[1], a1x, 1, ix, plane_peers, n_gx)
    pl.semaphore_wait(news.at[2], 2)
    value = stage(value, src1.at[2], a1z, 2, iy, z_peers, n_gy, boundary)

    gram = jnp.concatenate(
        [value[0:8]] + [pltpu.roll(value[0:8], 128 - 32 * k, 1) for k in range(1, 4)], axis=0
    )
    gram = jnp.where(eye_l < NV, gram, 0.0)
    proj = to_col(value[8:9], 0)
    mat = jnp.where(eye_l == eye_r + NV, 1.0, jnp.where(eye_l == 2 * NV, proj, gram))
    for k in range(0, NV, PIVOTS):
        cols = [jnp.broadcast_to(mat[:, k + j : k + j + 1], (NV, 128)) for j in range(PIVOTS)]
        rows = [mat[k + j : k + j + 1] for j in range(PIVOTS)]
        head = [[cols[j][k + i : k + i + 1] for j in range(PIVOTS)] for i in range(PIVOTS)]
        for j in range(PIVOTS):
            scaled = 1.0 / head[j][j]
            rows[j] = rows[j] * scaled
            for m in range(j + 1, PIVOTS):
                head[j][m] = head[j][m] * scaled
            for i in range(PIVOTS):
                if i != j:
                    rows[i] = rows[i] - head[i][j] * rows[j]
                    for m in range(j + 1, PIVOTS):
                        head[i][m] = head[i][m] - head[i][j] * head[j][m]
        for j in range(PIVOTS):
            mat = mat - cols[j] * rows[j]
        for j in range(PIVOTS):
            mat = jnp.where(eye_r == k + j, rows[j], mat)
    weights = mat[:, 2 * NV : 2 * NV + 1]
    inverse = jnp.where(jnp.logical_and(eye_l >= NV, eye_l < 2 * NV), mat, 0.0)
    wb[...] = jnp.broadcast_to(weights, (NV, 128))

    for copy in q_sends:
        copy.wait_recv()

    def scale(i):
        line = wb[i : i + 1, :]
        return jnp.concatenate([line, line], axis=1)

    guess = [zero for _ in range(BX)]
    halo = [zero for _ in range(4)]
    beyond = [qx[NV], qy[NV]]
    for i in range(NV):
        w = scale(i)
        for x in range(BX):
            guess[x] = guess[x] + w * v_ref[i, x]
        for at, ref in enumerate((hxlo, hxup, hylo, hyup)):
            halo[at] = halo[at] + w * ref[i]
        beyond = [beyond[0] - w * qx[i], beyond[1] - w * qy[i]]

    def apply(cells, hx_lo, hx_up, hy_lo, hy_up):
        hx_up = jnp.where(last_x, 0.0, hx_up)
        hy_up = jnp.where(last_y, 0.0, hy_up)
        before = cxlo_v * (hx_lo - cells[0])
        outs = []
        for x in range(BX):
            v = cells[x]
            flux = cf_ref[0, x] * (v - (cells[x + 1] if x < BX - 1 else hx_up))
            out = ext_ref[x] * v + flux - before
            before = flux
            v_up = jnp.where(row == BY - 1, hy_up[x : x + 1], pltpu.roll(v, BY - 1, 0))
            flux = cf_ref[1, x] * (v - v_up)
            below = cylo_v[x : x + 1] * (hy_lo[x : x + 1] - v)
            out = out + flux - jnp.where(row == 0, below, pltpu.roll(flux, 1, 0))
            v_up = jnp.where(lane == BZ - 1, 0.0, pltpu.roll(v, BZ - 1, 1))
            flux = cf_ref[2, x] * (v - v_up)
            out = out + flux - jnp.where(lane == 0, 0.0, pltpu.roll(flux, 1, 1))
            outs.append(out)
        return outs

    def apply_inside(cells):
        before = zero
        outs = []
        for x in range(BX):
            v = cells[x]
            flux = cxm[x] * (v - (cells[x + 1] if x < BX - 1 else zero))
            out = ext_ref[x] * v + flux - before
            before = flux
            flux = cym[x] * (v - turned(v, 0.0, 0.0)[1])
            out = out + flux - turned(flux, 0.0, 0.0)[0]
            flux = cf_ref[2, x] * (v - along_z(v)[1])
            out = out + flux - along_z(flux)[0]
            outs.append(out)
        return outs

    applied = apply(guess, *halo)
    rd = zero
    for x in range(BX):
        below = cxlo_v if x == 0 else cf_ref[0, x - 1]
        diagonal = ext_ref[x] + cf_ref[0, x] + cf_ref[1, x] + cf_ref[2, x] + below
        diagonal = diagonal + jnp.where(row == 0, cylo_v[x : x + 1], pltpu.roll(cf_ref[1, x], 1, 0))
        diagonal = diagonal + jnp.where(lane == 0, 0.0, pltpu.roll(cf_ref[2, x], 1, 1))
        res = rhs_ref[x] - applied[x]
        cell = res / diagonal
        d_ref[x] = cell
        rd = rd + res * cell
        g_ref[x] = 0.5 * guess[x]
    dplo[...] = d_ref[:, 0, :]
    dphi[...] = d_ref[:, BY - 1, :]

    cells = [d_ref[x] for x in range(BX)]
    applied = apply_inside(cells)
    jump_x = jnp.concatenate([cells[0][:, :HZ], cells[BX - 1][:, HZ:]], axis=1) - beyond[0]
    jump_y = jnp.concatenate([dplo[:, :HZ], dphi[:, HZ:]], axis=1) - beyond[1]
    flow_x, flow_y = cx_face * jump_x, cy_face * jump_y
    dad = flow_x * jump_x + flow_y * jump_y
    for x in range(BX):
        dad = dad + cells[x] * applied[x]

    def fold(block):
        return jnp.sum(block[:, :HZ] + block[:, HZ:], axis=0, keepdims=True)

    for i in range(NV):
        acc = v_ref[i, 0] * applied[0]
        for x in range(1, BX):
            acc = acc + v_ref[i, x] * applied[x]
        diff_x = [v_ref[i, 0, :, :HZ] - hxlo[i, :, :HZ], v_ref[i, BX - 1, :, HZ:] - hxup[i, :, HZ:]]
        diff_y = [pylo[i, :, :HZ] - hylo[i, :, :HZ], pyhi[i, :, HZ:] - hyup[i, :, HZ:]]
        acc = acc + flow_x * jnp.concatenate(diff_x, axis=1)
        acc = acc + flow_y * jnp.concatenate(diff_y, axis=1)
        proj_acc[i] = fold(acc)
    corr_col = jnp.sum(proj_acc[...].reshape(NV, HZ), axis=1, keepdims=True)
    line_at = lax.broadcasted_iota(jnp.int32, (1, 128), 1)
    value = to_row(corr_col, NV)
    value = jnp.where(line_at == 0, jnp.sum(fold(rd), axis=1, keepdims=True), value)
    value = jnp.where(line_at == 1, jnp.sum(fold(dad), axis=1, keepdims=True), value)
    kept = []

    def solve_rest():
        w_row = to_row(weights, 0)
        kept.append(proj - jnp.sum(gram * w_row, axis=1, keepdims=True))

    value = stage(value, src2.at[1], a2x, 4, ix, plane_peers, n_gx, solve_rest)
    rest = kept[0]
    value = stage(value, src2.at[2], a2z, 5, iy, z_peers, n_gy)

    shift = jnp.sum(inverse * value, axis=1, keepdims=True)
    wb[...] = jnp.broadcast_to(shift, (NV, 128))
    corr = to_col(value, NV)
    numerator = value[:, 0:1] - jnp.sum(shift * rest, axis=0, keepdims=True)
    denominator = value[:, 1:2] - jnp.sum(shift * corr, axis=0, keepdims=True)
    step = numerator / denominator
    update = [d_ref[x] for x in range(BX)]
    for i in range(NV):
        m = scale(i)
        for x in range(BX):
            update[x] = update[x] - m * v_ref[i, x]
    for x in range(BX):
        o_ref[x] = step * update[x]
    for copy in sent:
        copy.wait_send()
    for others, at in ar_waits:
        pltpu.make_async_copy(others, others, ar_send.at[at]).wait()


def solution(mesh):
    n_gx, n_gy = mesh.shape["gx"], mesh.shape["gy"]
    n_xy = n_gx // 2

    def on_device(basis, rhs, extra_diag, coeff):
        vm = pltpu.VMEM
        cell = (BX, BY, BZ)
        slab = (NV, 8, BZ)
        flat = (NV * BY, BX * BZ)
        face = (NV * BY, 2 * BZ)
        anywhere = pl.BlockSpec(memory_space=pl.ANY)
        half, change = pl.pallas_call(
            functools.partial(kernel, n_gx, n_gy),
            out_shape=[vm(cell, F32)] * 2,
            in_specs=[anywhere] * 4,
            out_specs=[pl.BlockSpec(memory_space=vm)] * 2,
            scratch_shapes=[
                vm((NV,) + cell, F32),
                vm(cell, F32),
                vm(cell, F32),
                vm((3,) + cell, F32),
            ]
            + [vm(flat, BF16)] * 4
            + [vm(face, BF16)] * 4
            + [vm(slab, F32)] * 6
            + [vm(cell, F32)] * 2
            + [vm((8, BZ), F32)] * 3
            + [
                vm((NV, 1, HZ), F32),
                vm((NV * BY, NV * BY), F32),
                vm((NV, 128), F32),
                vm(cell, F32),
            ]
            + [vm((8, BZ), F32)] * 2
            + [vm((4, 8, 8, BZ), F32)]
            + [vm((NV + 1, 8, BZ), F32)] * 4
            + [
                vm((3, ROWS, 128), F32),
                vm((3, 1, 128), F32),
                vm((n_gx, ROWS, 128), F32),
                vm((n_gy, ROWS, 128), F32),
                vm((n_gx, 1, 128), F32),
                vm((n_gy, 1, 128), F32),
                pltpu.SemaphoreType.DMA((CHUNKS + 3,)),
                pltpu.SemaphoreType.DMA((14,)),
                pltpu.SemaphoreType.DMA((14,)),
                pltpu.SemaphoreType.DMA((6,)),
                pltpu.SemaphoreType.DMA((6,)),
                pltpu.SemaphoreType.REGULAR((4,)),
                vm((4 * NV * BY, 128), BF16),
            ],
            compiler_params=pltpu.CompilerParams(
                collective_id=0, has_side_effects=True, vmem_limit_bytes=63 << 20
            ),
        )(basis, rhs, extra_diag, coeff)
        return 2.0 * half, 2.0 * half + change

    placed = (
        P(None, "gx", "gy", None),
        P("gx", "gy", None),
        P("gx", "gy", None),
        P(None, "gx", "gy", None),
    )
    return jax.shard_map(
        on_device,
        mesh=mesh,
        in_specs=placed,
        out_specs=(P("gx", "gy", None), P("gx", "gy", None)),
        check_vma=False,
    )
```
